32 devices in a mesh: gx: 4 (over z), gy: 4 (over y, x), gz: 2 (over core).
Axes of the slice: x: 2, y: 2, z: 4, core: 2. Of those that a mesh axis runs over, the one named last changes fastest.
Arguments:
- positions: float32 [3, 1536, 512], P(None, ('gx', 'gy', 'gz')), may hold values from -1 to 1
- spacing: float32 [1536, 8], P(('gx', 'gy', 'gz')), may hold values from 0.0005 to 0.02
- crossings: int32 [1536, 8], P(('gx', 'gy', 'gz')), may hold values from 0 to 31, all different within a row; in each aligned block of 48 rows (0 to 47, 48 to 95, ...) at most 24 rows name the same one
- target: float32 [3, 1536], P(None, ('gx', 'gy', 'gz')), may hold values from 0 to 1
- first_weight: bfloat16 [32, 256, 60], P(('gx', 'gy', 'gz')), may hold values from -0.75 to 0.75
- head_weight: bfloat16 [32, 4, 256], P(('gx', 'gy', 'gz')), may hold values from -0.375 to 0.375
Outputs:
- rendered: float32 [3, 1536], P(None, ('gx', 'gy', 'gz'))
- first_update: float32 [32, 256, 60], P(('gx', 'gy', 'gz'))
- head_update: float32 [32, 4, 256], P(('gx', 'gy', 'gz'))
The draws below stay inside these ranges and needn't reach their ends.
Inputs may be any that keep to these rules, and one draw needn't show every extreme that they name: `crossings`: each ray crosses 8 different bricks, in no spatial pattern over the devices. Among the rays of one device no brick is crossed more than 24 times, a bound that some block reaches.
All inputs are finite; a program needn't handle non-finite values.
Results may differ from the reference program's by a relative error of at most 0.0029.
Values sent between devices are 32-bit elements; how exact they have to be, the bound alone decides.
A program may use at most 64 MiB of HBM per device.

```python
import math
import jax
import jax.numpy as jnp
import numpy as np
from jax import lax

W = 256
FREQS = 10
SAMPLES = 64
SEGS = 8
RAY_DEV = 48
BRICKS = 32
RAYS = 1536
CAP = 24
DEVICES = 32


def block_scale(own_key, dims, pieces, low, top_value):
    gain = 1.0
    for position, shards_of in pieces:
        heights = jax.random.uniform(jax.random.fold_in(jax.random.fold_in(own_key, 6), position), (shards_of,), jnp.float32, low / len(pieces), top_value / len(pieces))
        gain = gain * jnp.repeat(jnp.exp(heights), dims[position] // shards_of).reshape((-1,) + (1,) * (len(dims) - 1 - position))
    return gain


def deal_out(rng, own, number, rows, number_of, top, limit, lean):
    order = jax.random.permutation(rng, number_of)
    heavy_load, common = load_shares(number_of, rows * top, limit, lean, True), load_shares(number_of, rows * top, limit, lean, False)
    places = jnp.arange(number_of)

    def named(tallies, turn):
        used = int((tallies > 0).sum())
        fixed = max(1, used // 4)
        moved = fixed + (places - fixed + turn * (used - fixed)) % max(1, number_of - fixed)
        return jnp.zeros((number_of,), jnp.int32).at[order[jnp.where(places < fixed, places, moved)]].set(jnp.asarray(tallies, jnp.int32))

    tallies = jnp.where(number % 4 == 0, named(heavy_load, number // 4), named(common, number - number // 4 - 1))
    mixed = jax.random.permutation(jax.random.fold_in(own, 3), number_of)
    donor, receiver = mixed[0:number_of // 2 * 2:2], mixed[1:number_of // 2 * 2:2]
    room = jnp.minimum(tallies[donor] - 1, limit - tallies[receiver]) // 2
    room = jnp.where((donor == order[0]) | (receiver == order[0]) | (tallies[receiver] == 0), 0, jnp.maximum(room, 0))
    moved = jax.random.randint(jax.random.fold_in(own, 4), (number_of // 2,), 0, 1 << 20) % (room + 1)
    tallies = tallies.at[donor].add(-moved).at[receiver].add(moved)
    labels = jnp.searchsorted(jnp.cumsum(tallies), jnp.arange(rows * top), side="right").astype(jnp.int32)
    listing = labels.reshape(top, rows).T
    listing = listing[jax.random.permutation(jax.random.fold_in(own, 1), rows)]
    turn = jax.random.randint(jax.random.fold_in(own, 2), (rows, 1), 0, top)
    return jnp.take_along_axis(listing, (jnp.arange(top)[None, :] + turn) % top, axis=1)


def load_shares(amount, total, bound, lean, full):
    portions = [(1 << 20) // math.isqrt(standing ** lean) + 1 for standing in range(1, amount + 1)]
    largest = bound if full else min(bound, max(-(-total // amount), total * portions[0] // sum(portions)))
    least = 1 if total - largest >= amount - 1 else 0
    counts, rest = [largest] + [least] * (amount - 1), total - largest - least * (amount - 1)
    while rest > 0:
        free = [i for i in range(1, amount) if counts[i] < largest] or [i for i in range(1, amount) if counts[i] < bound]
        mass, left = sum([portions[i] for i in free]), rest
        for i in free:
            addition = min(bound - counts[i], max(1, left * portions[i] // mass), rest)
            counts[i] = counts[i] + addition
            rest = rest - addition
    return np.array(counts)


def bell_draw(own_key, extent, scale, most, split=(), kind=jnp.bfloat16):
    values = jax.random.normal(own_key, extent, jnp.float32) * scale
    if len(split) > 0:
        values = block_scale(own_key, extent, split, -0.22, 0.18) * values
    return jnp.clip(values, min=-most, max=most).astype(kind)


def setup_inputs(seed: int = 0) -> dict:
    keys = jax.random.split(jax.random.key(seed), 7)
    positions = jnp.clip(jax.random.uniform(keys[0], (3, RAYS, SEGS * SAMPLES), jnp.float32, -1.0, 1.0) * block_scale(keys[0], (3, RAYS, SEGS * SAMPLES), ((1, 32),), -0.4, 0.0), -1.0, 1.0)
    spacing = jnp.clip(jnp.exp(math.log(0.02) - 3.6888794 * jax.random.uniform(keys[1], (RAYS, SEGS), jnp.float32) ** block_scale(keys[1], (RAYS, SEGS), ((0, 32),), -0.2, 0.2)), 0.0005, 0.02)
    crossings_keys = jax.random.split(jax.random.fold_in(keys[2], 1), RAYS // RAY_DEV)
    crossings_turns = jax.random.permutation(jax.random.fold_in(keys[2], 3), RAYS // RAY_DEV)
    crossings = jax.vmap(lambda own, number: deal_out(jax.random.fold_in(keys[2], 2), own, number, RAY_DEV, DEVICES, SEGS, CAP, 2))(crossings_keys, crossings_turns).reshape((RAYS, SEGS))
    target = jnp.clip(1.0 * jax.random.uniform(keys[3], (3, RAYS), jnp.float32) ** block_scale(keys[3], (3, RAYS), ((1, 32),), -0.2, 0.2), 0.0, 1.0)
    first_weight = bell_draw(keys[4], (BRICKS, W, 6 * FREQS), (6 * FREQS) ** -0.5, 0.75, ((0, 32),))
    head_weight = bell_draw(keys[5], (BRICKS, 4, W), W ** -0.5, 0.375, ((0, 32),))
    return {"positions": positions, "spacing": spacing, "crossings": crossings, "target": target, "first_weight": first_weight, "head_weight": head_weight}


PI_VALUE = 3.141592653589793
NORM_EPS = 1e-06

def encode(points):
    scales = 2.0 ** jnp.arange(FREQS, dtype=jnp.float32) * PI_VALUE
    angles = scales[:, None, None] * points[None]
    wave_table = jnp.stack([jnp.sin(angles), jnp.cos(angles)], axis=1)
    return wave_table.reshape(6 * FREQS, points.shape[1]).astype(jnp.bfloat16)

def network(first_local, head_local, points):
    encoded = encode(points)
    before = jnp.dot(first_local, encoded, preferred_element_type=jnp.float32)
    hidden = jax.nn.silu(before).astype(jnp.bfloat16)
    output = jnp.dot(head_local, hidden, preferred_element_type=jnp.float32)
    return (encoded, before, hidden, output)

def activate(output):
    return (jax.nn.softplus(output[0]), jax.nn.sigmoid(output[1:]))

def segment_forward(density, colour, step_len):
    optical = density * step_len[:, None]
    inclusive = jnp.cumsum(optical, axis=1)
    leaving = jnp.exp(-inclusive)
    weight = jnp.exp(optical - inclusive) - leaving
    seg_colour = lax.optimization_barrier(jnp.sum(weight[None] * colour, axis=2))
    return (seg_colour, leaving[:, -1], weight, leaving)

def segment_backward(colour, weight, leaving, step_len, grad_colour, grad_trans):
    shading = lax.optimization_barrier(jnp.sum(colour * grad_colour[:, :, None], axis=0))
    weighted = weight * shading
    after = lax.optimization_barrier(jnp.sum(weighted, axis=1, keepdims=True)) - jnp.cumsum(weighted, axis=1)
    grad_depth = shading * leaving - after - (grad_trans * leaving[:, -1])[:, None]
    grad_density = grad_depth * step_len[:, None]
    grad_sample = weight[None] * grad_colour[:, :, None]
    return (grad_density, grad_sample)

def ray_level(seg_colour, seg_trans, target):
    seg_total = seg_trans.shape[1]
    through = jnp.cumprod(seg_trans, axis=1)
    prefix = jnp.concatenate([jnp.ones_like(seg_trans[:, :1]), through[:, :-1]], axis=1)
    rendered = lax.optimization_barrier(jnp.sum(prefix[None] * seg_colour, axis=2))
    residual = rendered - target
    grad_colour = prefix[None] * residual[:, :, None]
    behind_list = [jnp.zeros_like(rendered)]
    for offset in range(seg_total - 1, 0, -1):
        behind_list.append(seg_colour[:, :, offset] + seg_trans[:, offset][None] * behind_list[-1])
    behind = jnp.stack(behind_list[::-1], axis=2)
    grad_trans = prefix * lax.optimization_barrier(jnp.sum(behind * residual[:, :, None], axis=0))
    return (rendered, grad_colour, grad_trans)

def output_grad(output, grad_density, grad_sample):
    colour = jax.nn.sigmoid(output[1:])
    first_row = grad_density * jax.nn.sigmoid(output[0])
    others = grad_sample * colour * (1.0 - colour)
    return jnp.concatenate([first_row[None], others], axis=0).astype(jnp.bfloat16)

def network_grad(head_local, encoded, before, hidden, upstream):
    grad_head = jnp.dot(upstream, hidden.T, preferred_element_type=jnp.float32)
    grad_hidden = jnp.dot(head_local.T, upstream, preferred_element_type=jnp.float32)
    logistic = jax.nn.sigmoid(before)
    grad_before = (grad_hidden * logistic * (1.0 + before * (1.0 - logistic))).astype(jnp.bfloat16)
    grad_first = jnp.dot(grad_before, encoded.T, preferred_element_type=jnp.float32)
    return (grad_first, grad_head)

def reference(positions, spacing, crossings, target, first_weight, head_weight):
    entries = RAY_DEV * SEGS
    brick_ids = crossings.reshape(BRICKS, entries)
    order_rank = jnp.arange(entries, dtype=jnp.int32)

    def rank_row(row):
        earlier = (row[:, None] == row[None, :]) & (order_rank[None, :] < order_rank[:, None])
        return lax.optimization_barrier(jnp.sum(earlier.astype(jnp.int32), axis=1))
    local_slot = jax.vmap(rank_row)(brick_ids).astype(jnp.int32)
    owner_ids = jnp.arange(BRICKS, dtype=jnp.int32)[:, None]
    column = ((brick_ids * BRICKS + owner_ids) * CAP + local_slot).reshape(RAYS * SEGS).astype(jnp.int32)
    brick_slots = BRICKS * CAP
    all_slots = BRICKS * brick_slots
    all_points = jnp.zeros((3, all_slots, SAMPLES), jnp.float32).at[:, column, :].set(positions.reshape(3, RAYS * SEGS, SAMPLES))
    brick_points = all_points.reshape(3, BRICKS, brick_slots * SAMPLES).transpose(1, 0, 2)

    def brick_forward(inputs):
        first_local, head_local, points = inputs
        return network(first_local, head_local, points)[3]
    outputs = lax.map(brick_forward, (first_weight, head_weight, brick_points))
    entry_out = outputs.reshape(BRICKS, 4, brick_slots, SAMPLES).transpose(1, 0, 2, 3).reshape(4, all_slots, SAMPLES)[:, column, :]
    density, colour = activate(entry_out)
    steps_all = spacing.reshape(RAYS * SEGS)
    seg_colour, seg_trans, weight, leaving = segment_forward(density, colour, steps_all)
    rendered, grad_colour, grad_trans = ray_level(seg_colour.reshape(3, RAYS, SEGS), seg_trans.reshape(RAYS, SEGS), target)
    grad_density, grad_sample = segment_backward(colour, weight, leaving, steps_all, grad_colour.reshape(3, RAYS * SEGS), grad_trans.reshape(RAYS * SEGS))
    upstream = output_grad(entry_out, grad_density, grad_sample)
    brick_upstream = jnp.zeros((4, all_slots, SAMPLES), jnp.bfloat16).at[:, column, :].set(upstream)
    brick_upstream = brick_upstream.reshape(4, BRICKS, brick_slots * SAMPLES).transpose(1, 0, 2)

    def brick_backward(inputs):
        first_local, head_local, points, upstream_local = inputs
        encoded, before, hidden, output = network(first_local, head_local, points)
        return network_grad(head_local, encoded, before, hidden, upstream_local)
    grad_first, grad_head = lax.map(brick_backward, (first_weight, head_weight, brick_points, brick_upstream))
    overall = jnp.sum(grad_first * grad_first) + jnp.sum(grad_head * grad_head)
    scale = lax.rsqrt(overall / (BRICKS * W * (6 * FREQS + 4)) + NORM_EPS)
    return (rendered, grad_first * scale, grad_head * scale)
```

```python
import functools
import math

import jax
import jax.numpy as jnp
from jax import lax
from jax.experimental import pallas as pl
from jax.experimental.pallas import tpu as pltpu
from jax.sharding import PartitionSpec as P

FREQS = 10
SAMPLES = 64
SEGS = 8
AXES = ("gx", "gy", "gz")
ENC = 6 * FREQS
ROWS = ENC + 4
HID = 256
PACK = 4
LANES = PACK * SAMPLES
GATHER_LIMIT = 64
VMEM_BYTES = 58 * 1024 * 1024
HIGHEST = lax.Precision.HIGHEST


PI_VALUE = 3.141592653589793
NORM_EPS = 1e-06
BLOCK_LIMIT = 2048


def exact_dot(a, b):
    return jnp.dot(a, b, precision=HIGHEST, preferred_element_type=jnp.float32)


def iota(shape, dim):
    return lax.broadcasted_iota(jnp.int32, shape, dim)


def logistic(x):
    return 0.5 + 0.5 * jnp.tanh(0.5 * x)


def encode_block(p0, p1, p2):
    shape = (ROWS, LANES)
    row = iota((ROWS, 1), 0)
    freq = row // 6
    wave = row % 6 // 3
    axis = row % 3
    scale = jnp.zeros((ROWS, 1), jnp.float32)
    for k in range(FREQS):
        scale = jnp.where(freq == k, 2.0**k, scale)
    point = jnp.where(
        axis == 0,
        jnp.broadcast_to(p0, shape),
        jnp.where(axis == 1, jnp.broadcast_to(p1, shape), jnp.broadcast_to(p2, shape)),
    )
    turns = point * scale
    whole = jnp.round(turns)
    rest = turns - whole
    odd = jnp.abs(whole - 2.0 * jnp.round(0.5 * whole))
    sign = 1.0 - 2.0 * odd
    is_cos = (wave == 1) & (row < ENC)
    arg = jnp.where(is_cos, 0.5 - jnp.abs(rest), rest)
    square = arg * arg
    total = jnp.full(shape, -(PI_VALUE**11) / math.factorial(11), jnp.float32)
    for power in (9, 7, 5, 3, 1):
        factor = PI_VALUE**power / math.factorial(power)
        total = total * square + (factor if power % 4 == 1 else -factor)
    return (total * arg * sign).astype(jnp.bfloat16)


def rays_kernel(
    groups,
    bricks,
    ray_rows,
    brick_of,
    weights,
    staged,
    group_row,
    group_col,
    place_col,
    target,
    rendered_out,
    grads,
    weight_t,
    encoded,
    hidden,
    slope,
    points,
    outs,
    ups,
    per_entry,
):
    entries = ray_rows * SEGS
    turns = (brick_of[groups] + 1) // 2

    place = (iota((groups, entries), 0) == group_row[...]).astype(jnp.float32)
    for c in range(4):
        points[c] = exact_dot(place, staged[c])
    outs[...] = jnp.zeros_like(outs)
    grads[...] = jnp.zeros_like(grads)

    @pl.loop(0, bricks)
    def _(b):
        weight_t[b] = weights[b].T.astype(jnp.bfloat16)

    def forward(g):
        b = brick_of[g]
        enc = encode_block(*[points[c, pl.ds(g, 1), :] for c in range(3)])
        encoded[g] = enc
        before = jnp.dot(weight_t[b], enc, preferred_element_type=jnp.float32)
        sig = logistic(before)
        act = before * sig
        slope[g] = (sig + act * (1.0 - sig)).astype(jnp.bfloat16)
        hid = act.astype(jnp.bfloat16)
        hidden[g] = hid
        head = weights[b, ROWS - 8 :, :].astype(jnp.bfloat16)
        out = jnp.dot(head, hid, preferred_element_type=jnp.float32)
        for ch in range(4):
            outs[ch, pl.ds(g, 1), :] = out[4 + ch : 5 + ch, :]

    @pl.loop(0, turns)
    def _(turn):
        forward(2 * turn)
        forward(2 * turn + 1)

    same = iota((LANES, LANES), 0) // SAMPLES == iota((LANES, LANES), 1) // SAMPLES
    upto = (same & (iota((LANES, LANES), 0) <= iota((LANES, LANES), 1))).astype(jnp.float32)
    beyond = (same & (iota((LANES, LANES), 0) > iota((LANES, LANES), 1))).astype(jnp.float32)
    steps = points[3]
    raw = outs[0]
    density = jnp.maximum(raw, 0.0) + jnp.log1p(jnp.exp(-jnp.abs(raw)))
    colour = [logistic(outs[1 + c]) for c in range(3)]
    optical = density * steps
    inclusive = exact_dot(optical, upto)
    leaving = jnp.exp(-inclusive)
    weight = jnp.exp(optical - inclusive) - leaving
    lane = iota((LANES, 128), 0)
    col = iota((LANES, 128), 1)
    sums = jnp.zeros((groups, 128), jnp.float32)
    for ch in range(4):
        pick = col == 4 * ch + lane // SAMPLES
        if ch == 3:
            pick = pick & (lane % SAMPLES == SAMPLES - 1)
        sums = sums + exact_dot(weight * colour[ch] if ch < 3 else leaving, pick.astype(jnp.float32))
    back = (iota((entries, groups), 1) == group_col[...]).astype(jnp.float32)
    found = exact_dot(back, sums)
    entry_col = iota((entries, 128), 1)
    here = entry_col % 4 == place_col[...]
    values = [
        jnp.sum(jnp.where(here & (entry_col // 4 == ch), found, 0.0), axis=1, keepdims=True)
        for ch in range(4)
    ]

    def seg(ch, s):
        return values[ch][s * ray_rows : (s + 1) * ray_rows]

    prefix = [jnp.ones((ray_rows, 1), jnp.float32)]
    for s in range(SEGS - 1):
        prefix.append(prefix[s] * seg(3, s))
    residual = []
    for c in range(3):
        shown = sum(prefix[s] * seg(c, s) for s in range(SEGS))
        rendered_out[c] = shown
        residual.append(shown - target[c])
    behind = [jnp.zeros((ray_rows, 1), jnp.float32)] * 3
    for s in range(SEGS - 1, -1, -1):
        grad_trans = prefix[s] * sum(behind[c] * residual[c] for c in range(3))
        rows = pl.ds(s * ray_rows, ray_rows)
        mine = here[s * ray_rows : (s + 1) * ray_rows]
        which = entry_col[s * ray_rows : (s + 1) * ray_rows] // 4
        block = jnp.zeros((ray_rows, 128), jnp.float32)
        for ch in range(4):
            value = prefix[s] * residual[ch] if ch < 3 else grad_trans * seg(3, s)
            block = jnp.where(mine & (which == ch), value, block)
        per_entry[rows, :] = block
        behind = [seg(c, s) + seg(3, s) * behind[c] for c in range(3)]
    spread = exact_dot(place, per_entry[...])
    wide = []
    for ch in range(4):
        to_lanes = iota((128, LANES), 0) == 4 * ch + iota((128, LANES), 1) // SAMPLES
        wide.append(exact_dot(spread, to_lanes.astype(jnp.float32)))
    shading = sum(colour[c] * wide[c] for c in range(3))
    after = exact_dot(weight * shading, beyond)
    ups[0] = (shading * leaving - after - wide[3]) * steps * logistic(raw)
    for c in range(3):
        ups[1 + c] = weight * wide[c] * colour[c] * (1.0 - colour[c])

    row8 = iota((8, LANES), 0)

    def backward(g):
        b = brick_of[g]
        up8 = jnp.zeros((8, LANES), jnp.float32)
        for ch in range(4):
            line = jnp.broadcast_to(ups[ch, pl.ds(g, 1), :], (8, LANES))
            up8 = jnp.where(row8 == 4 + ch, line, up8)
        up = jnp.concatenate([jnp.zeros((ROWS - 8, LANES), jnp.float32), up8], axis=0)
        up = up.astype(jnp.bfloat16)
        grad_hidden = jnp.dot(weight_t[b], up, preferred_element_type=jnp.float32)
        grad_before = (grad_hidden * slope[g].astype(jnp.float32)).astype(jnp.bfloat16)
        dims = (((1,), (1,)), ((), ()))
        return lax.dot_general(
            encoded[g], grad_before, dims, preferred_element_type=jnp.float32
        ) + lax.dot_general(up, hidden[g], dims, preferred_element_type=jnp.float32)

    @pl.loop(0, turns)
    def _(turn):
        first = backward(2 * turn)
        second = backward(2 * turn + 1)
        grads[brick_of[2 * turn]] += first
        grads[brick_of[2 * turn + 1]] += second


def own_rays(positions, spacing, crossings, target, gathered):
    bricks = gathered.shape[0]
    ray_rows = crossings.shape[0]
    entries = ray_rows * SEGS
    groups = -(-((entries + (PACK - 1) * bricks) // PACK) // 8) * 8
    brick_ids = crossings.T.reshape(entries)
    order_rank = jnp.arange(entries, dtype=jnp.int32)
    earlier = (brick_ids[:, None] == brick_ids[None, :]) & (
        order_rank[None, :] < order_rank[:, None]
    )
    rank = jnp.sum(earlier.astype(jnp.int32), axis=1)
    all_bricks = jnp.arange(bricks, dtype=jnp.int32)
    counts = jnp.sum((brick_ids[:, None] == all_bricks[None, :]).astype(jnp.int32), axis=0)
    needed = (counts + PACK - 1) // PACK
    ends = jnp.sum(
        jnp.where(all_bricks[None, :] <= all_bricks[:, None], needed[None, :], 0), axis=1
    )
    start = jnp.sum(
        jnp.where(all_bricks[None, :] < brick_ids[:, None], needed[None, :], 0), axis=1
    )
    group = start + rank // PACK
    place = rank % PACK
    numbers = jnp.arange(groups, dtype=jnp.int32)
    brick_of = jnp.minimum(
        jnp.sum((ends[None, :] <= numbers[:, None]).astype(jnp.int32), axis=1), bricks - 1
    )
    brick_of = jnp.concatenate([brick_of, jnp.sum(needed)[None]])
    points = positions.reshape(3, ray_rows, SEGS, 1, SAMPLES).transpose(0, 2, 1, 3, 4)
    steps = jnp.broadcast_to(spacing.T[None, :, :, None, None], (1, SEGS, ray_rows, 1, SAMPLES))
    values = jnp.concatenate([points, steps], axis=0).reshape(4, entries, 1, SAMPLES)
    chosen = place[None, :, None, None] == jnp.arange(PACK, dtype=jnp.int32)[None, None, :, None]
    staged = jnp.where(chosen, values, 0.0).reshape(4, entries, LANES)
    vmem = pl.BlockSpec(memory_space=pltpu.VMEM)
    samples = groups * LANES
    rendered, grads = pl.pallas_call(
        functools.partial(rays_kernel, groups, bricks, ray_rows),
        out_shape=(
            jax.ShapeDtypeStruct((3, ray_rows, 1), jnp.float32),
            jax.ShapeDtypeStruct((bricks, ROWS, HID), jnp.float32),
        ),
        in_specs=[pl.BlockSpec(memory_space=pltpu.SMEM)] + [vmem] * 6,
        out_specs=(vmem, vmem),
        scratch_shapes=[
            pltpu.VMEM((bricks, HID, ROWS), jnp.bfloat16),
            pltpu.VMEM((groups, ROWS, LANES), jnp.bfloat16),
            pltpu.VMEM((groups, HID, LANES), jnp.bfloat16),
            pltpu.VMEM((groups, HID, LANES), jnp.bfloat16),
            pltpu.VMEM((4, groups, LANES), jnp.float32),
            pltpu.VMEM((4, groups, LANES), jnp.float32),
            pltpu.VMEM((4, groups, LANES), jnp.float32),
            pltpu.VMEM((entries, 128), jnp.float32),
        ],
        compiler_params=pltpu.CompilerParams(vmem_limit_bytes=VMEM_BYTES),
        cost_estimate=pl.CostEstimate(
            flops=samples * HID * ROWS * 10,
            transcendentals=samples * HID,
            bytes_accessed=2 * bricks * ROWS * HID * 4,
        ),
        name="own_rays",
    )(
        brick_of,
        gathered,
        staged,
        group[None, :],
        group[:, None],
        place[:, None],
        target[:, :, None],
    )
    return rendered[:, :, 0], grads


def by_gather(positions, spacing, crossings, target, first_weight, head_weight):
    devices = lax.axis_size(AXES)
    packed = jnp.concatenate(
        [first_weight[0].astype(jnp.float32).T, head_weight[0].astype(jnp.float32)], axis=0
    )
    gathered = lax.all_gather(packed, AXES, axis=0, tiled=False)
    rendered, grads = own_rays(positions, spacing, crossings, target, gathered)
    total = lax.psum_scatter(grads, AXES, scatter_dimension=0, tiled=False)
    overall = lax.psum(jnp.sum(total * total), AXES)
    scale = lax.rsqrt(overall / (devices * total.size) + NORM_EPS)
    scaled = total * scale
    return (rendered, scaled[:ENC].T[None], scaled[ENC:][None])


def encode(points):
    scales = 2.0 ** jnp.arange(FREQS, dtype=jnp.float32) * PI_VALUE
    angles = scales[:, None, None] * points[None]
    wave_table = jnp.stack([jnp.sin(angles), jnp.cos(angles)], axis=1)
    return wave_table.reshape(6 * FREQS, points.shape[1]).astype(jnp.bfloat16)


def network(first_local, head_local, points):
    encoded = encode(points)
    before = jnp.dot(first_local, encoded, preferred_element_type=jnp.float32)
    hidden = jax.nn.silu(before).astype(jnp.bfloat16)
    output = jnp.dot(head_local, hidden, preferred_element_type=jnp.float32)
    return (encoded, before, hidden, output)


def activate(output):
    return (jax.nn.softplus(output[0]), jax.nn.sigmoid(output[1:]))


def segment_forward(density, colour, step_len):
    optical = density * step_len[:, None]
    inclusive = jnp.cumsum(optical, axis=1)
    leaving = jnp.exp(-inclusive)
    weight = jnp.exp(optical - inclusive) - leaving
    seg_colour = jnp.sum(weight[None] * colour, axis=2)
    return (seg_colour, leaving[:, -1], weight, leaving)


def segment_backward(colour, weight, leaving, step_len, grad_colour, grad_trans):
    shading = jnp.sum(colour * grad_colour[:, :, None], axis=0)
    weighted = weight * shading
    after = jnp.sum(weighted, axis=1, keepdims=True) - jnp.cumsum(weighted, axis=1)
    grad_depth = shading * leaving - after - (grad_trans * leaving[:, -1])[:, None]
    grad_density = grad_depth * step_len[:, None]
    grad_sample = weight[None] * grad_colour[:, :, None]
    return (grad_density, grad_sample)


def ray_level(seg_colour, seg_trans, target):
    seg_total = seg_trans.shape[1]
    through = jnp.cumprod(seg_trans, axis=1)
    prefix = jnp.concatenate([jnp.ones_like(seg_trans[:, :1]), through[:, :-1]], axis=1)
    rendered = jnp.sum(prefix[None] * seg_colour, axis=2)
    residual = rendered - target
    grad_colour = prefix[None] * residual[:, :, None]
    behind_list = [jnp.zeros_like(rendered)]
    for offset in range(seg_total - 1, 0, -1):
        behind_list.append(seg_colour[:, :, offset] + seg_trans[:, offset][None] * behind_list[-1])
    behind = jnp.stack(behind_list[::-1], axis=2)
    grad_trans = prefix * jnp.sum(behind * residual[:, :, None], axis=0)
    return (rendered, grad_colour, grad_trans)


def output_grad(output, grad_density, grad_sample):
    colour = jax.nn.sigmoid(output[1:])
    first_row = grad_density * jax.nn.sigmoid(output[0])
    others = grad_sample * colour * (1.0 - colour)
    return jnp.concatenate([first_row[None], others], axis=0).astype(jnp.bfloat16)


def network_grad(head_local, encoded, before, hidden, upstream):
    grad_head = lax.dot_general(
        upstream, hidden, (((1,), (1,)), ((), ())), preferred_element_type=jnp.float32
    )
    grad_hidden = lax.dot_general(
        head_local, upstream, (((0,), (0,)), ((), ())), preferred_element_type=jnp.float32
    )
    logistic = jax.nn.sigmoid(before)
    grad_before = (grad_hidden * logistic * (1.0 + before * (1.0 - logistic))).astype(jnp.bfloat16)
    grad_first = lax.dot_general(
        grad_before, encoded, (((1,), (1,)), ((), ())), preferred_element_type=jnp.float32
    )
    return (grad_first, grad_head)


def by_exchange(positions, spacing, crossings, target, first_weight, head_weight):
    across = lax.axis_size(("gx", "gy"))
    along_count = lax.axis_size("gz")
    devices = across * along_count
    ray_rows = crossings.shape[0]
    entries = ray_rows * SEGS
    capacity = 2 * entries // devices
    total_slots = devices * capacity
    sample_total = total_slots * SAMPLES
    block_size = math.gcd(sample_total, BLOCK_LIMIT)
    block_count = sample_total // block_size
    block_segs = block_size // SAMPLES
    first_local = first_weight[0]
    head_local = head_weight[0]
    brick_ids = crossings.reshape(entries)
    order_rank = jnp.arange(entries, dtype=jnp.int32)
    earlier = (brick_ids[:, None] == brick_ids[None, :]) & (
        order_rank[None, :] < order_rank[:, None]
    )
    column = brick_ids * capacity + jnp.sum(earlier.astype(jnp.int32), axis=1)
    own_points = positions.reshape(3, entries, SAMPLES)
    own_steps = spacing.reshape(entries)
    send_points = jnp.zeros((3, total_slots, SAMPLES), jnp.float32).at[:, column, :].set(own_points)
    send_steps = jnp.zeros((1, total_slots), jnp.float32).at[0, column].set(own_steps)
    got_points, got_steps = (
        lax.all_to_all(
            lax.all_to_all(
                send_points.reshape(3, across, along_count, capacity * SAMPLES),
                ("gx", "gy"),
                split_axis=1,
                concat_axis=1,
                tiled=True,
            ),
            "gz",
            split_axis=2,
            concat_axis=2,
            tiled=True,
        ),
        lax.all_to_all(
            lax.all_to_all(
                send_steps.reshape(1, across, along_count, capacity),
                ("gx", "gy"),
                split_axis=1,
                concat_axis=1,
                tiled=True,
            ),
            "gz",
            split_axis=2,
            concat_axis=2,
            tiled=True,
        ),
    )
    point_blocks = got_points.reshape(3, block_count, block_size).transpose(1, 0, 2)
    step_blocks = got_steps.reshape(block_count, block_segs)

    def forward_turn(unused, inputs):
        block_points, block_steps = inputs
        encoded, before, hidden, output = network(first_local, head_local, block_points)
        density, colour = activate(output)
        result = jnp.concatenate([density[None], colour], axis=0)
        return (unused, result)

    unused, results = lax.scan(
        forward_turn, jnp.zeros((), jnp.float32), (point_blocks, step_blocks)
    )
    values = results.transpose(1, 0, 2).reshape(4, across, along_count, capacity * SAMPLES)
    returned = lax.all_to_all(
        lax.all_to_all(values, ("gx", "gy"), split_axis=1, concat_axis=1, tiled=True),
        "gz",
        split_axis=2,
        concat_axis=2,
        tiled=True,
    )
    owned = returned.reshape(4, total_slots, SAMPLES)[:, column, :]
    seg_colour, seg_trans, weight, leaving = segment_forward(owned[0], owned[1:], own_steps)
    rendered, grad_colour, grad_trans = ray_level(
        seg_colour.reshape(3, ray_rows, SEGS), seg_trans.reshape(ray_rows, SEGS), target
    )
    grad_density, grad_sample = segment_backward(
        owned[1:],
        weight,
        leaving,
        own_steps,
        grad_colour.reshape(3, entries),
        grad_trans.reshape(entries),
    )
    stacked = jnp.concatenate([grad_density[None], grad_sample], axis=0)
    send_grads = jnp.zeros((4, total_slots, SAMPLES), jnp.float32).at[:, column, :].set(stacked)
    got_grads = lax.all_to_all(
        lax.all_to_all(
            send_grads.reshape(4, across, along_count, capacity * SAMPLES),
            ("gx", "gy"),
            split_axis=1,
            concat_axis=1,
            tiled=True,
        ),
        "gz",
        split_axis=2,
        concat_axis=2,
        tiled=True,
    )
    grad_blocks = got_grads.reshape(4, block_count, block_size).transpose(1, 0, 2)

    def backward_turn(totals, inputs):
        block_points, block_steps, block_upstream = inputs
        encoded, before, hidden, output = network(first_local, head_local, block_points)
        grad_density = block_upstream[0]
        grad_sample = block_upstream[1:]
        upstream = output_grad(output, grad_density, grad_sample)
        grad_first, grad_head = network_grad(head_local, encoded, before, hidden, upstream)
        return ((totals[0] + grad_first, totals[1] + grad_head), None)

    start_totals = (
        jnp.zeros(first_local.shape, jnp.float32),
        jnp.zeros(head_local.shape, jnp.float32),
    )
    totals, unused_out = lax.scan(
        backward_turn, start_totals, (point_blocks, step_blocks, grad_blocks)
    )
    grad_first, grad_head = totals
    square_sum = jnp.sum(grad_first * grad_first) + jnp.sum(grad_head * grad_head)
    overall = lax.psum(square_sum, ("gx", "gy", "gz"))
    count_all = devices * (grad_first.size + grad_head.size)
    scale = lax.rsqrt(overall / count_all + NORM_EPS)
    return (rendered, (grad_first * scale)[None], (grad_head * scale)[None])


def solution(mesh):
    in_specs = (
        P(None, ("gx", "gy", "gz"), None),
        P(("gx", "gy", "gz"), None),
        P(("gx", "gy", "gz"), None),
        P(None, ("gx", "gy", "gz")),
        P(("gx", "gy", "gz"), None, None),
        P(("gx", "gy", "gz"), None, None),
    )
    out_specs = (
        P(None, ("gx", "gy", "gz")),
        P(("gx", "gy", "gz"), None, None),
        P(("gx", "gy", "gz"), None, None),
    )
    body = by_gather if mesh.size <= GATHER_LIMIT else by_exchange
    return jax.shard_map(
        body, mesh=mesh, in_specs=in_specs, out_specs=out_specs, check_vma=False
    )
```

```python
import functools
import math

import jax
import jax.numpy as jnp
from jax import lax
from jax.experimental import pallas as pl
from jax.experimental.pallas import tpu as pltpu
from jax.sharding import PartitionSpec as P

FREQS = 10
SAMPLES = 64
SEGS = 8
AXES = ("gx", "gy", "gz")
ENC = 6 * FREQS
ROWS = ENC + 4
HID = 256
PACK = 4
LANES = PACK * SAMPLES
GATHER_LIMIT = 64
VMEM_BYTES = 58 * 1024 * 1024
HIGHEST = lax.Precision.HIGHEST


PI_VALUE = 3.141592653589793
NORM_EPS = 1e-06
BLOCK_LIMIT = 2048


def exact_dot(a, b):
    return jnp.dot(a, b, precision=HIGHEST, preferred_element_type=jnp.float32)


def iota(shape, dim):
    return lax.broadcasted_iota(jnp.int32, shape, dim)


def logistic(x):
    return 0.5 + 0.5 * jnp.tanh(0.5 * x)


def encode_block(p0, p1, p2):
    shape = (ROWS, LANES)
    row = iota((ROWS, 1), 0)
    freq = row // 6
    wave = row % 6 // 3
    axis = row % 3
    scale = jnp.zeros((ROWS, 1), jnp.float32)
    for k in range(FREQS):
        scale = jnp.where(freq == k, 2.0**k, scale)
    point = jnp.where(
        axis == 0,
        jnp.broadcast_to(p0, shape),
        jnp.where(axis == 1, jnp.broadcast_to(p1, shape), jnp.broadcast_to(p2, shape)),
    )
    turns = point * scale
    whole = jnp.round(turns)
    rest = turns - whole
    odd = jnp.abs(whole - 2.0 * jnp.round(0.5 * whole))
    sign = 1.0 - 2.0 * odd
    is_cos = (wave == 1) & (row < ENC)
    arg = jnp.where(is_cos, 0.5 - jnp.abs(rest), rest)
    square = arg * arg
    total = jnp.full(shape, -(PI_VALUE**11) / math.factorial(11), jnp.float32)
    for power in (9, 7, 5, 3, 1):
        factor = PI_VALUE**power / math.factorial(power)
        total = total * square + (factor if power % 4 == 1 else -factor)
    return (total * arg * sign).astype(jnp.bfloat16)


def rays_kernel(
    groups,
    bricks,
    ray_rows,
    brick_of,
    weights,
    staged,
    group_row,
    group_col,
    place_col,
    target,
    rendered_out,
    grads,
    weight_t,
    encoded,
    hidden,
    slope,
    points,
    outs,
    ups,
    per_entry,
):
    entries = ray_rows * SEGS
    turns = (brick_of[groups] + 1) // 2

    place = (iota((groups, entries), 0) == group_row[...]).astype(jnp.float32)
    for c in range(4):
        points[c] = exact_dot(place, staged[c])
    outs[...] = jnp.zeros_like(outs)
    grads[...] = jnp.zeros_like(grads)

    @pl.loop(0, bricks)
    def _(b):
        weight_t[b] = weights[b].T.astype(jnp.bfloat16)

    def forward(g):
        b = brick_of[g]
        enc = encode_block(*[points[c, pl.ds(g, 1), :] for c in range(3)])
        encoded[g] = enc
        before = jnp.dot(weight_t[b], enc, preferred_element_type=jnp.float32)
        sig = logistic(before)
        act = before * sig
        slope[g] = (sig + act * (1.0 - sig)).astype(jnp.bfloat16)
        hid = act.astype(jnp.bfloat16)
        hidden[g] = hid
        head = weights[b, ROWS - 8 :, :].astype(jnp.bfloat16)
        out = jnp.dot(head, hid, preferred_element_type=jnp.float32)
        for ch in range(4):
            outs[ch, pl.ds(g, 1), :] = out[4 + ch : 5 + ch, :]

    @pl.loop(0, turns)
    def _(turn):
        forward(2 * turn)
        forward(2 * turn + 1)

    same = iota((LANES, LANES), 0) // SAMPLES == iota((LANES, LANES), 1) // SAMPLES
    upto = (same & (iota((LANES, LANES), 0) <= iota((LANES, LANES), 1))).astype(jnp.float32)
    beyond = (same & (iota((LANES, LANES), 0) > iota((LANES, LANES), 1))).astype(jnp.float32)
    steps = points[3]
    raw = outs[0]
    density = jnp.maximum(raw, 0.0) + jnp.log1p(jnp.exp(-jnp.abs(raw)))
    colour = [logistic(outs[1 + c]) for c in range(3)]
    optical = density * steps
    inclusive = exact_dot(optical, upto)
    leaving = jnp.exp(-inclusive)
    weight = jnp.exp(optical - inclusive) - leaving
    lane = iota((LANES, 128), 0)
    col = iota((LANES, 128), 1)
    sums = jnp.zeros((groups, 128), jnp.float32)
    for ch in range(4):
        pick = col == 4 * ch + lane // SAMPLES
        if ch == 3:
            pick = pick & (lane % SAMPLES == SAMPLES - 1)
        sums = sums + exact_dot(weight * colour[ch] if ch < 3 else leaving, pick.astype(jnp.float32))
    back = (iota((entries, groups), 1) == group_col[...]).astype(jnp.float32)
    found = exact_dot(back, sums)
    entry_col = iota((entries, 128), 1)
    here = entry_col % 4 == place_col[...]
    values = [
        jnp.sum(jnp.where(here & (entry_col // 4 == ch), found, 0.0), axis=1, keepdims=True)
        for ch in range(4)
    ]

    def seg(ch, s):
        return values[ch][s * ray_rows : (s + 1) * ray_rows]

    prefix = [jnp.ones((ray_rows, 1), jnp.float32)]
    for s in range(SEGS - 1):
        prefix.append(prefix[s] * seg(3, s))
    residual = []
    for c in range(3):
        shown = sum(prefix[s] * seg(c, s) for s in range(SEGS))
        rendered_out[c] = shown
        residual.append(shown - target[c])
    behind = [jnp.zeros((ray_rows, 1), jnp.float32)] * 3
    for s in range(SEGS - 1, -1, -1):
        grad_trans = prefix[s] * sum(behind[c] * residual[c] for c in range(3))
        rows = pl.ds(s * ray_rows, ray_rows)
        mine = here[s * ray_rows : (s + 1) * ray_rows]
        which = entry_col[s * ray_rows : (s + 1) * ray_rows] // 4
        block = jnp.zeros((ray_rows, 128), jnp.float32)
        for ch in range(4):
            value = prefix[s] * residual[ch] if ch < 3 else grad_trans * seg(3, s)
            block = jnp.where(mine & (which == ch), value, block)
        per_entry[rows, :] = block
        behind = [seg(c, s) + seg(3, s) * behind[c] for c in range(3)]
    spread = exact_dot(place, per_entry[...])
    wide = []
    for ch in range(4):
        to_lanes = iota((128, LANES), 0) == 4 * ch + iota((128, LANES), 1) // SAMPLES
        wide.append(exact_dot(spread, to_lanes.astype(jnp.float32)))
    shading = sum(colour[c] * wide[c] for c in range(3))
    after = exact_dot(weight * shading, beyond)
    ups[0] = (shading * leaving - after - wide[3]) * steps * logistic(raw)
    for c in range(3):
        ups[1 + c] = weight * wide[c] * colour[c] * (1.0 - colour[c])

    row8 = iota((8, LANES), 0)

    def backward(g):
        b = brick_of[g]
        up8 = jnp.zeros((8, LANES), jnp.float32)
        for ch in range(4):
            line = jnp.broadcast_to(ups[ch, pl.ds(g, 1), :], (8, LANES))
            up8 = jnp.where(row8 == 4 + ch, line, up8)
        up = jnp.concatenate([jnp.zeros((ROWS - 8, LANES), jnp.float32), up8], axis=0)
        up = up.astype(jnp.bfloat16)
        grad_hidden = jnp.dot(weight_t[b], up, preferred_element_type=jnp.float32)
        grad_before = (grad_hidden * slope[g].astype(jnp.float32)).astype(jnp.bfloat16)
        dims = (((1,), (1,)), ((), ()))
        return lax.dot_general(
            encoded[g], grad_before, dims, preferred_element_type=jnp.float32
        ) + lax.dot_general(up, hidden[g], dims, preferred_element_type=jnp.float32)

    @pl.loop(0, turns)
    def _(turn):
        first = backward(2 * turn)
        second = backward(2 * turn + 1)
        grads[brick_of[2 * turn]] += first
        grads[brick_of[2 * turn + 1]] += second


def own_rays(positions, spacing, crossings, target, gathered):
    bricks = gathered.shape[0]
    ray_rows = crossings.shape[0]
    entries = ray_rows * SEGS
    groups = -(-((entries + (PACK - 1) * bricks) // PACK) // 8) * 8
    brick_ids = crossings.T.reshape(entries)
    order_rank = jnp.arange(entries, dtype=jnp.int32)
    earlier = (brick_ids[:, None] == brick_ids[None, :]) & (
        order_rank[None, :] < order_rank[:, None]
    )
    rank = jnp.sum(earlier.astype(jnp.int32), axis=1)
    all_bricks = jnp.arange(bricks, dtype=jnp.int32)
    counts = jnp.sum((brick_ids[:, None] == all_bricks[None, :]).astype(jnp.int32), axis=0)
    needed = (counts + PACK - 1) // PACK
    ends = jnp.sum(
        jnp.where(all_bricks[None, :] <= all_bricks[:, None], needed[None, :], 0), axis=1
    )
    start = jnp.sum(
        jnp.where(all_bricks[None, :] < brick_ids[:, None], needed[None, :], 0), axis=1
    )
    group = start + rank // PACK
    place = rank % PACK
    numbers = jnp.arange(groups, dtype=jnp.int32)
    brick_of = jnp.minimum(
        jnp.sum((ends[None, :] <= numbers[:, None]).astype(jnp.int32), axis=1), bricks - 1
    )
    brick_of = jnp.concatenate([brick_of, jnp.sum(needed)[None]])
    points = positions.reshape(3, ray_rows, SEGS, 1, SAMPLES).transpose(0, 2, 1, 3, 4)
    steps = jnp.broadcast_to(spacing.T[None, :, :, None, None], (1, SEGS, ray_rows, 1, SAMPLES))
    values = jnp.concatenate([points, steps], axis=0).reshape(4, entries, 1, SAMPLES)
    chosen = place[None, :, None, None] == jnp.arange(PACK, dtype=jnp.int32)[None, None, :, None]
    staged = jnp.where(chosen, values, 0.0).reshape(4, entries, LANES)
    vmem = pl.BlockSpec(memory_space=pltpu.VMEM)
    samples = groups * LANES
    rendered, grads = pl.pallas_call(
        functools.partial(rays_kernel, groups, bricks, ray_rows),
        out_shape=(
            jax.ShapeDtypeStruct((3, ray_rows, 1), jnp.float32),
            jax.ShapeDtypeStruct((bricks, ROWS, HID), jnp.float32),
        ),
        in_specs=[pl.BlockSpec(memory_space=pltpu.SMEM)] + [vmem] * 6,
        out_specs=(vmem, vmem),
        scratch_shapes=[
            pltpu.VMEM((bricks, HID, ROWS), jnp.bfloat16),
            pltpu.VMEM((groups, ROWS, LANES), jnp.bfloat16),
            pltpu.VMEM((groups, HID, LANES), jnp.bfloat16),
            pltpu.VMEM((groups, HID, LANES), jnp.bfloat16),
            pltpu.VMEM((4, groups, LANES), jnp.float32),
            pltpu.VMEM((4, groups, LANES), jnp.float32),
            pltpu.VMEM((4, groups, LANES), jnp.float32),
            pltpu.VMEM((entries, 128), jnp.float32),
        ],
        compiler_params=pltpu.CompilerParams(vmem_limit_bytes=VMEM_BYTES),
        cost_estimate=pl.CostEstimate(
            flops=samples * HID * ROWS * 10,
            transcendentals=samples * HID,
            bytes_accessed=2 * bricks * ROWS * HID * 4,
        ),
        name="own_rays",
    )(
        brick_of,
        gathered,
        staged,
        group[None, :],
        group[:, None],
        place[:, None],
        target[:, :, None],
    )
    return rendered[:, :, 0], grads


def partners(sizes):
    here = tuple(lax.axis_index(name) for name in AXES)

    def shifted(axis, step):
        place = list(here)
        place[axis] = lax.rem(here[axis] + step, sizes[axis])
        return tuple(place)

    others = [shifted(axis, step) for axis in range(3) for step in range(1, sizes[axis])]
    return here, shifted, others


def greet(others):
    barrier = pltpu.get_barrier_semaphore()
    for other in others:
        pl.semaphore_signal(barrier, inc=1, device_id=other, device_id_type=pl.DeviceIdType.MESH)
    pl.semaphore_wait(barrier, len(others))


def transfer(source, landing, send_sem, recv_sem, device):
    return pltpu.make_async_remote_copy(
        src_ref=source,
        dst_ref=landing,
        send_sem=send_sem,
        recv_sem=recv_sem,
        device_id=device,
        device_id_type=pl.DeviceIdType.MESH,
    )


def gather_kernel(sizes, own, out, sends, recvs):
    nx, ny, nz = sizes
    (x, y, z), shifted, others = partners(sizes)
    greet(others)
    out[x, y, z] = own[...]
    started = []

    def block(dx, dy, dz):
        return out.at[
            lax.rem(x - dx + nx, nx), lax.rem(y - dy + ny, ny), lax.rem(z - dz + nz, nz)
        ]

    def send(source, axis, step, came):
        where = (came[0] * ny + came[1]) * nz + came[2]
        copy = transfer(source, source, sends.at[where], recvs.at[where], shifted(axis, step))
        copy.start()
        started.append(copy)

    def arrive(came):
        where = (came[0] * ny + came[1]) * nz + came[2]
        landed = block(*came)
        transfer(landed, landed, sends.at[where], recvs.at[where], others[0]).wait_recv()

    for dx in range(1, nx):
        send(block(0, 0, 0), 0, dx, (dx, 0, 0))
    for dx in range(nx):
        if dx > 0:
            arrive((dx, 0, 0))
        for dy in range(1, ny):
            send(block(dx, 0, 0), 1, dy, (dx, dy, 0))
        for dz in range(1, nz):
            send(block(dx, 0, 0), 2, dz, (dx, 0, dz))
    for dx in range(nx):
        for dy in range(1, ny):
            arrive((dx, dy, 0))
            for dz in range(1, nz):
                send(block(dx, dy, 0), 2, dz, (dx, dy, dz))
    for dx in range(nx):
        for dy in range(ny):
            for dz in range(1, nz):
                arrive((dx, dy, dz))
    for copy in started:
        copy.wait_send()


def gather_weights(packed, sizes):
    count = sizes[0] * sizes[1] * sizes[2]
    vmem = pl.BlockSpec(memory_space=pltpu.VMEM)
    gathered = pl.pallas_call(
        functools.partial(gather_kernel, sizes),
        out_shape=jax.ShapeDtypeStruct(sizes + packed.shape, jnp.float32),
        in_specs=[vmem],
        out_specs=vmem,
        scratch_shapes=[pltpu.SemaphoreType.DMA((count,)), pltpu.SemaphoreType.DMA((count,))],
        compiler_params=pltpu.CompilerParams(
            collective_id=0, has_side_effects=True, vmem_limit_bytes=VMEM_BYTES
        ),
        name="gather_weights",
    )(packed)
    return gathered.reshape((count,) + packed.shape)


def update_kernel(
    sizes, grads, out, from_z, sum_z, from_y, sum_y, from_x, parts, sends, recvs, small_s, small_r
):
    nx, ny, nz = sizes
    (x, y, z), shifted, others = partners(sizes)
    greet(others)
    started = []

    def place(step, axis):
        return lax.rem((x, y, z)[axis] + step, sizes[axis])

    def number(step):
        return (step[0] * ny + step[1]) * nz + step[2]

    def send(source, landing, where, axis, step):
        copy = transfer(source, landing, sends.at[where], recvs.at[where], shifted(axis, step))
        copy.start()
        started.append(copy)

    def arrive(landing, where):
        transfer(landing, landing, sends.at[where], recvs.at[where], others[0]).wait_recv()

    order_x = list(range(1, nx)) + [0]
    order_y = list(range(1, ny)) + [0]
    for dx in order_x:
        for dy in order_y:
            for dz in range(1, nz):
                send(
                    grads.at[place(dx, 0), place(dy, 1), place(dz, 2)],
                    from_z.at[dx, dy, dz - 1],
                    number((dx, dy, dz)),
                    2,
                    dz,
                )
    for dx in order_x:
        for dy in order_y:
            total = grads[place(dx, 0), place(dy, 1), z]
            for dz in range(1, nz):
                arrive(from_z.at[dx, dy, dz - 1], number((dx, dy, dz)))
                total = total + from_z[dx, dy, dz - 1]
            sum_z[dx, dy] = total
            if dy > 0:
                send(sum_z.at[dx, dy], from_y.at[dx, dy - 1], number((dx, dy, 0)), 1, dy)
    for dx in order_x:
        total = sum_z[dx, 0]
        for dy in range(1, ny):
            arrive(from_y.at[dx, dy - 1], number((dx, dy, 0)))
            total = total + from_y[dx, dy - 1]
        sum_y[dx] = total
        if dx > 0:
            send(sum_y.at[dx], from_x.at[dx - 1], number((dx, 0, 0)), 0, dx)
    for dx in range(1, nx):
        arrive(from_x.at[dx - 1], number((dx, 0, 0)))
        total = total + from_x[dx - 1]
    square = total * total
    part = jnp.zeros((8, 128), jnp.float32)
    for i in range(0, square.shape[0], 8):
        for j in range(0, square.shape[1], 128):
            part = part + square[i : i + 8, j : j + 128]
    slot = 0
    for axis in range(3):
        parts[slot] = part
        copies = []
        for step in range(1, sizes[axis]):
            copy = transfer(
                parts.at[slot],
                parts.at[slot + step],
                small_s.at[slot + step],
                small_r.at[slot + step],
                shifted(axis, step),
            )
            copy.start()
            copies.append(copy)
        for step in range(1, sizes[axis]):
            copies[step - 1].wait_recv()
            part = part + parts[slot + step]
        started.extend(copies)
        slot += sizes[axis]
    overall = jnp.sum(part, keepdims=True)
    count_all = nx * ny * nz * total.size
    out[...] = total * lax.rsqrt(overall / count_all + NORM_EPS)
    for copy in started:
        copy.wait_send()


def sum_and_scale(grads, sizes):
    nx, ny, nz = sizes
    count = nx * ny * nz
    tile = grads.shape[1:]
    vmem = pl.BlockSpec(memory_space=pltpu.VMEM)
    small = nx + ny + nz
    return pl.pallas_call(
        functools.partial(update_kernel, sizes),
        out_shape=jax.ShapeDtypeStruct(tile, jnp.float32),
        in_specs=[vmem],
        out_specs=vmem,
        scratch_shapes=[
            pltpu.VMEM((nx, ny, max(nz - 1, 1)) + tile, jnp.float32),
            pltpu.VMEM((nx, ny) + tile, jnp.float32),
            pltpu.VMEM((nx, max(ny - 1, 1)) + tile, jnp.float32),
            pltpu.VMEM((nx,) + tile, jnp.float32),
            pltpu.VMEM((max(nx - 1, 1),) + tile, jnp.float32),
            pltpu.VMEM((small, 8, 128), jnp.float32),
            pltpu.SemaphoreType.DMA((count,)),
            pltpu.SemaphoreType.DMA((count,)),
            pltpu.SemaphoreType.DMA((small,)),
            pltpu.SemaphoreType.DMA((small,)),
        ],
        compiler_params=pltpu.CompilerParams(
            collective_id=1, has_side_effects=True, vmem_limit_bytes=VMEM_BYTES
        ),
        name="sum_and_scale",
    )(grads.reshape(sizes + tile))


def by_gather(positions, spacing, crossings, target, first_weight, head_weight):
    sizes = tuple(lax.axis_size(name) for name in AXES)
    packed = jnp.concatenate(
        [first_weight[0].astype(jnp.float32).T, head_weight[0].astype(jnp.float32)], axis=0
    )
    gathered = gather_weights(packed, sizes)
    rendered, grads = own_rays(positions, spacing, crossings, target, gathered)
    scaled = sum_and_scale(grads, sizes)
    return (rendered, scaled[:ENC].T[None], scaled[ENC:][None])


def encode(points):
    scales = 2.0 ** jnp.arange(FREQS, dtype=jnp.float32) * PI_VALUE
    angles = scales[:, None, None] * points[None]
    wave_table = jnp.stack([jnp.sin(angles), jnp.cos(angles)], axis=1)
    return wave_table.reshape(6 * FREQS, points.shape[1]).astype(jnp.bfloat16)


def network(first_local, head_local, points):
    encoded = encode(points)
    before = jnp.dot(first_local, encoded, preferred_element_type=jnp.float32)
    hidden = jax.nn.silu(before).astype(jnp.bfloat16)
    output = jnp.dot(head_local, hidden, preferred_element_type=jnp.float32)
    return (encoded, before, hidden, output)


def activate(output):
    return (jax.nn.softplus(output[0]), jax.nn.sigmoid(output[1:]))


def segment_forward(density, colour, step_len):
    optical = density * step_len[:, None]
    inclusive = jnp.cumsum(optical, axis=1)
    leaving = jnp.exp(-inclusive)
    weight = jnp.exp(optical - inclusive) - leaving
    seg_colour = jnp.sum(weight[None] * colour, axis=2)
    return (seg_colour, leaving[:, -1], weight, leaving)


def segment_backward(colour, weight, leaving, step_len, grad_colour, grad_trans):
    shading = jnp.sum(colour * grad_colour[:, :, None], axis=0)
    weighted = weight * shading
    after = jnp.sum(weighted, axis=1, keepdims=True) - jnp.cumsum(weighted, axis=1)
    grad_depth = shading * leaving - after - (grad_trans * leaving[:, -1])[:, None]
    grad_density = grad_depth * step_len[:, None]
    grad_sample = weight[None] * grad_colour[:, :, None]
    return (grad_density, grad_sample)


def ray_level(seg_colour, seg_trans, target):
    seg_total = seg_trans.shape[1]
    through = jnp.cumprod(seg_trans, axis=1)
    prefix = jnp.concatenate([jnp.ones_like(seg_trans[:, :1]), through[:, :-1]], axis=1)
    rendered = jnp.sum(prefix[None] * seg_colour, axis=2)
    residual = rendered - target
    grad_colour = prefix[None] * residual[:, :, None]
    behind_list = [jnp.zeros_like(rendered)]
    for offset in range(seg_total - 1, 0, -1):
        behind_list.append(seg_colour[:, :, offset] + seg_trans[:, offset][None] * behind_list[-1])
    behind = jnp.stack(behind_list[::-1], axis=2)
    grad_trans = prefix * jnp.sum(behind * residual[:, :, None], axis=0)
    return (rendered, grad_colour, grad_trans)


def output_grad(output, grad_density, grad_sample):
    colour = jax.nn.sigmoid(output[1:])
    first_row = grad_density * jax.nn.sigmoid(output[0])
    others = grad_sample * colour * (1.0 - colour)
    return jnp.concatenate([first_row[None], others], axis=0).astype(jnp.bfloat16)


def network_grad(head_local, encoded, before, hidden, upstream):
    grad_head = lax.dot_general(
        upstream, hidden, (((1,), (1,)), ((), ())), preferred_element_type=jnp.float32
    )
    grad_hidden = lax.dot_general(
        head_local, upstream, (((0,), (0,)), ((), ())), preferred_element_type=jnp.float32
    )
    logistic = jax.nn.sigmoid(before)
    grad_before = (grad_hidden * logistic * (1.0 + before * (1.0 - logistic))).astype(jnp.bfloat16)
    grad_first = lax.dot_general(
        grad_before, encoded, (((1,), (1,)), ((), ())), preferred_element_type=jnp.float32
    )
    return (grad_first, grad_head)


def by_exchange(positions, spacing, crossings, target, first_weight, head_weight):
    across = lax.axis_size(("gx", "gy"))
    along_count = lax.axis_size("gz")
    devices = across * along_count
    ray_rows = crossings.shape[0]
    entries = ray_rows * SEGS
    capacity = 2 * entries // devices
    total_slots = devices * capacity
    sample_total = total_slots * SAMPLES
    block_size = math.gcd(sample_total, BLOCK_LIMIT)
    block_count = sample_total // block_size
    block_segs = block_size // SAMPLES
    first_local = first_weight[0]
    head_local = head_weight[0]
    brick_ids = crossings.reshape(entries)
    order_rank = jnp.arange(entries, dtype=jnp.int32)
    earlier = (brick_ids[:, None] == brick_ids[None, :]) & (
        order_rank[None, :] < order_rank[:, None]
    )
    column = brick_ids * capacity + jnp.sum(earlier.astype(jnp.int32), axis=1)
    own_points = positions.reshape(3, entries, SAMPLES)
    own_steps = spacing.reshape(entries)
    send_points = jnp.zeros((3, total_slots, SAMPLES), jnp.float32).at[:, column, :].set(own_points)
    send_steps = jnp.zeros((1, total_slots), jnp.float32).at[0, column].set(own_steps)
    got_points, got_steps = (
        lax.all_to_all(
            lax.all_to_all(
                send_points.reshape(3, across, along_count, capacity * SAMPLES),
                ("gx", "gy"),
                split_axis=1,
                concat_axis=1,
                tiled=True,
            ),
            "gz",
            split_axis=2,
            concat_axis=2,
            tiled=True,
        ),
        lax.all_to_all(
            lax.all_to_all(
                send_steps.reshape(1, across, along_count, capacity),
                ("gx", "gy"),
                split_axis=1,
                concat_axis=1,
                tiled=True,
            ),
            "gz",
            split_axis=2,
            concat_axis=2,
            tiled=True,
        ),
    )
    point_blocks = got_points.reshape(3, block_count, block_size).transpose(1, 0, 2)
    step_blocks = got_steps.reshape(block_count, block_segs)

    def forward_turn(unused, inputs):
        block_points, block_steps = inputs
        encoded, before, hidden, output = network(first_local, head_local, block_points)
        density, colour = activate(output)
        result = jnp.concatenate([density[None], colour], axis=0)
        return (unused, result)

    unused, results = lax.scan(
        forward_turn, jnp.zeros((), jnp.float32), (point_blocks, step_blocks)
    )
    values = results.transpose(1, 0, 2).reshape(4, across, along_count, capacity * SAMPLES)
    returned = lax.all_to_all(
        lax.all_to_all(values, ("gx", "gy"), split_axis=1, concat_axis=1, tiled=True),
        "gz",
        split_axis=2,
        concat_axis=2,
        tiled=True,
    )
    owned = returned.reshape(4, total_slots, SAMPLES)[:, column, :]
    seg_colour, seg_trans, weight, leaving = segment_forward(owned[0], owned[1:], own_steps)
    rendered, grad_colour, grad_trans = ray_level(
        seg_colour.reshape(3, ray_rows, SEGS), seg_trans.reshape(ray_rows, SEGS), target
    )
    grad_density, grad_sample = segment_backward(
        owned[1:],
        weight,
        leaving,
        own_steps,
        grad_colour.reshape(3, entries),
        grad_trans.reshape(entries),
    )
    stacked = jnp.concatenate([grad_density[None], grad_sample], axis=0)
    send_grads = jnp.zeros((4, total_slots, SAMPLES), jnp.float32).at[:, column, :].set(stacked)
    got_grads = lax.all_to_all(
        lax.all_to_all(
            send_grads.reshape(4, across, along_count, capacity * SAMPLES),
            ("gx", "gy"),
            split_axis=1,
            concat_axis=1,
            tiled=True,
        ),
        "gz",
        split_axis=2,
        concat_axis=2,
        tiled=True,
    )
    grad_blocks = got_grads.reshape(4, block_count, block_size).transpose(1, 0, 2)

    def backward_turn(totals, inputs):
        block_points, block_steps, block_upstream = inputs
        encoded, before, hidden, output = network(first_local, head_local, block_points)
        grad_density = block_upstream[0]
        grad_sample = block_upstream[1:]
        upstream = output_grad(output, grad_density, grad_sample)
        grad_first, grad_head = network_grad(head_local, encoded, before, hidden, upstream)
        return ((totals[0] + grad_first, totals[1] + grad_head), None)

    start_totals = (
        jnp.zeros(first_local.shape, jnp.float32),
        jnp.zeros(head_local.shape, jnp.float32),
    )
    totals, unused_out = lax.scan(
        backward_turn, start_totals, (point_blocks, step_blocks, grad_blocks)
    )
    grad_first, grad_head = totals
    square_sum = jnp.sum(grad_first * grad_first) + jnp.sum(grad_head * grad_head)
    overall = lax.psum(square_sum, ("gx", "gy", "gz"))
    count_all = devices * (grad_first.size + grad_head.size)
    scale = lax.rsqrt(overall / count_all + NORM_EPS)
    return (rendered, (grad_first * scale)[None], (grad_head * scale)[None])


def solution(mesh):
    in_specs = (
        P(None, ("gx", "gy", "gz"), None),
        P(("gx", "gy", "gz"), None),
        P(("gx", "gy", "gz"), None),
        P(None, ("gx", "gy", "gz")),
        P(("gx", "gy", "gz"), None, None),
        P(("gx", "gy", "gz"), None, None),
    )
    out_specs = (
        P(None, ("gx", "gy", "gz")),
        P(("gx", "gy", "gz"), None, None),
        P(("gx", "gy", "gz"), None, None),
    )
    body = by_gather if mesh.size <= GATHER_LIMIT else by_exchange
    return jax.shard_map(
        body, mesh=mesh, in_specs=in_specs, out_specs=out_specs, check_vma=False
    )
```

```python
import functools
import math

import jax
import jax.numpy as jnp
from jax import lax
from jax.experimental import pallas as pl
from jax.experimental.pallas import tpu as pltpu
from jax.sharding import PartitionSpec as P

FREQS = 10
SAMPLES = 64
SEGS = 8
AXES = ("gx", "gy", "gz")
ENC = 6 * FREQS
ROWS = ENC + 4
HID = 256
PACK = 4
LANES = PACK * SAMPLES
GATHER_LIMIT = 64
VMEM_BYTES = 58 * 1024 * 1024
HIGHEST = lax.Precision.HIGHEST


PI_VALUE = 3.141592653589793
NORM_EPS = 1e-06
BLOCK_LIMIT = 2048


def exact_dot(a, b):
    return jnp.dot(a, b, precision=HIGHEST, preferred_element_type=jnp.float32)


def iota(shape, dim):
    return lax.broadcasted_iota(jnp.int32, shape, dim)


def logistic(x):
    return 0.5 + 0.5 * jnp.tanh(0.5 * x)


def encode_block(p0, p1, p2):
    shape = (ROWS, LANES)
    row = iota((ROWS, 1), 0)
    freq = row // 6
    wave = row % 6 // 3
    axis = row % 3
    scale = jnp.zeros((ROWS, 1), jnp.float32)
    for k in range(FREQS):
        scale = jnp.where(freq == k, 2.0**k, scale)
    point = jnp.where(
        axis == 0,
        jnp.broadcast_to(p0, shape),
        jnp.where(axis == 1, jnp.broadcast_to(p1, shape), jnp.broadcast_to(p2, shape)),
    )
    turns = point * scale
    whole = jnp.round(turns)
    rest = turns - whole
    odd = jnp.abs(whole - 2.0 * jnp.round(0.5 * whole))
    sign = 1.0 - 2.0 * odd
    is_cos = (wave == 1) & (row < ENC)
    arg = jnp.where(is_cos, 0.5 - jnp.abs(rest), rest)
    square = arg * arg
    total = jnp.full(shape, -(PI_VALUE**11) / math.factorial(11), jnp.float32)
    for power in (9, 7, 5, 3, 1):
        factor = PI_VALUE**power / math.factorial(power)
        total = total * square + (factor if power % 4 == 1 else -factor)
    return (total * arg * sign).astype(jnp.bfloat16)


def to_column(row):
    n = row.shape[1]
    return jnp.sum(jnp.where(iota((n, n), 0) == iota((n, n), 1), row, 0.0), axis=1, keepdims=True)


def to_row(column):
    n = column.shape[0]
    return jnp.sum(
        jnp.where(iota((n, n), 0) == iota((n, n), 1), column, 0.0), axis=0, keepdims=True
    )


def number_groups(bricks, crossings, group_row, group_col, place_col, brick_of):
    ids_col = jnp.concatenate(
        [to_column(crossings[s : s + 1, :].astype(jnp.float32)) for s in range(SEGS)], axis=0
    )
    entries = ids_col.shape[0]
    ids_row = to_row(ids_col)
    square = (entries, entries)
    same = ids_col == ids_row
    rank_col = jnp.sum(
        jnp.where(same & (iota(square, 1) < iota(square, 0)), 1.0, 0.0), axis=1, keepdims=True
    )
    rank_row = jnp.sum(
        jnp.where(same & (iota(square, 0) < iota(square, 1)), 1.0, 0.0), axis=0, keepdims=True
    )
    wide = 128
    of_brick = ids_col == iota((entries, wide), 1).astype(jnp.float32)
    counts = jnp.sum(jnp.where(of_brick, 1.0, 0.0), axis=0, keepdims=True)
    needed_row = jnp.floor((counts + (PACK - 1)) * (1.0 / PACK))
    needed_col = to_column(needed_row)
    pair = (wide, wide)
    start_row = jnp.sum(
        jnp.where(iota(pair, 0) < iota(pair, 1), needed_col, 0.0), axis=0, keepdims=True
    )
    start_col = to_column(start_row)
    first_col = jnp.sum(jnp.where(of_brick, start_row, 0.0), axis=1, keepdims=True)
    of_brick_t = ids_row == iota((wide, entries), 0).astype(jnp.float32)
    first_row = jnp.sum(jnp.where(of_brick_t, start_col, 0.0), axis=0, keepdims=True)
    full_col = jnp.floor(rank_col * (1.0 / PACK))
    full_row = jnp.floor(rank_row * (1.0 / PACK))
    group_col[...] = (first_col + full_col).astype(jnp.int32)
    group_row[...] = (first_row + full_row).astype(jnp.int32)
    place_col[...] = (rank_col - PACK * full_col).astype(jnp.int32)
    shape = (wide, brick_of.shape[1])
    number = iota(shape, 1).astype(jnp.float32)
    passed = (start_col + needed_col <= number) & (iota(shape, 0) < bricks)
    found = jnp.sum(jnp.where(passed, 1.0, 0.0), axis=0, keepdims=True)
    total = jnp.sum(needed_row, axis=1, keepdims=True)
    last = iota(brick_of.shape, 1) == brick_of.shape[1] - 1
    brick_of[...] = jnp.where(last, total, jnp.minimum(found, bricks - 1.0)).astype(jnp.int32)


def place_points(groups, positions, spacing, group_row, place_col, points, steps):
    ray_rows = positions.shape[1]
    entries = ray_rows * SEGS
    place = (iota((groups, entries), 0) == group_row[...]).astype(jnp.float32)
    chosen = place_col[...] == iota((entries, LANES), 1) // SAMPLES
    low = iota((ray_rows, 2 * SAMPLES), 1) < SAMPLES
    for c in range(3):
        parts = []
        for pair in range(SEGS // 2):
            both = positions[c, :, 2 * SAMPLES * pair : 2 * SAMPLES * (pair + 1)]
            turned = pltpu.roll(both, SAMPLES, 1)
            for half in (jnp.where(low, both, turned), jnp.where(low, turned, both)):
                parts.append(jnp.concatenate([half] * (LANES // (2 * SAMPLES)), axis=1))
        values = jnp.where(chosen, jnp.concatenate(parts, axis=0), 0.0)
        points[c] = exact_dot(place, values)
    lengths = jnp.concatenate(
        [to_column(spacing[s : s + 1, :]) for s in range(SEGS)], axis=0
    )
    steps[...] = exact_dot(place, jnp.where(chosen, lengths, 0.0))


def rays_kernel(
    groups,
    bricks,
    ray_rows,
    brick_list,
    weights,
    encoded,
    steps_in,
    group_row,
    group_col,
    place_col,
    target,
    rendered_out,
    grads,
    weight_t,
    hidden,
    slope,
    outs,
    ups,
    per_entry,
):
    entries = ray_rows * SEGS
    together = 4
    turns = (brick_list[0, brick_list.shape[1] - 1] + together - 1) // together
    place = (iota((groups, entries), 0) == group_row[...]).astype(jnp.float32)
    outs[...] = jnp.zeros_like(outs)
    grads[...] = jnp.zeros_like(grads)

    few = math.gcd(bricks, 4)

    @pl.loop(0, bricks // few)
    def _(turn):
        for i in range(few):
            weight_t[few * turn + i] = weights[few * turn + i].T.astype(jnp.bfloat16)

    def forward(g):
        b = brick_list[0, g]
        before = jnp.dot(weight_t[b], encoded[g], preferred_element_type=jnp.float32)
        sig = logistic(before)
        act = before * sig
        slope[g] = (sig + act * (1.0 - sig)).astype(jnp.bfloat16)
        hid = act.astype(jnp.bfloat16)
        hidden[g] = hid
        head = weights[b, ROWS - 8 :, :].astype(jnp.bfloat16)
        out = jnp.dot(head, hid, preferred_element_type=jnp.float32)
        for ch in range(4):
            outs[ch, pl.ds(g, 1), :] = out[4 + ch : 5 + ch, :]

    @pl.loop(0, turns)
    def _(turn):
        for i in range(together):
            forward(together * turn + i)

    same = iota((LANES, LANES), 0) // SAMPLES == iota((LANES, LANES), 1) // SAMPLES
    upto = (same & (iota((LANES, LANES), 0) <= iota((LANES, LANES), 1))).astype(jnp.float32)
    beyond = (same & (iota((LANES, LANES), 0) > iota((LANES, LANES), 1))).astype(jnp.float32)
    steps = steps_in[...]
    raw = outs[0]
    density = jnp.maximum(raw, 0.0) + jnp.log1p(jnp.exp(-jnp.abs(raw)))
    colour = [logistic(outs[1 + c]) for c in range(3)]
    optical = density * steps
    inclusive = exact_dot(optical, upto)
    leaving = jnp.exp(-inclusive)
    weight = jnp.exp(optical - inclusive) - leaving
    lane = iota((LANES, 128), 0)
    col = iota((LANES, 128), 1)
    sums = jnp.zeros((groups, 128), jnp.float32)
    for ch in range(4):
        pick = col == 4 * ch + lane // SAMPLES
        if ch == 3:
            pick = pick & (lane % SAMPLES == SAMPLES - 1)
        sums = sums + exact_dot(weight * colour[ch] if ch < 3 else leaving, pick.astype(jnp.float32))
    back = (iota((entries, groups), 1) == group_col[...]).astype(jnp.float32)
    found = exact_dot(back, sums)
    entry_col = iota((entries, 128), 1)
    here = entry_col % 4 == place_col[...]
    values = [
        jnp.sum(jnp.where(here & (entry_col // 4 == ch), found, 0.0), axis=1, keepdims=True)
        for ch in range(4)
    ]

    def seg(ch, s):
        return values[ch][s * ray_rows : (s + 1) * ray_rows]

    prefix = [jnp.ones((ray_rows, 1), jnp.float32)]
    for s in range(SEGS - 1):
        prefix.append(prefix[s] * seg(3, s))
    residual = []
    for c in range(3):
        shown = sum(prefix[s] * seg(c, s) for s in range(SEGS))
        rendered_out[c : c + 1, :] = to_row(shown)
        residual.append(shown - to_column(target[c : c + 1, :]))
    behind = [jnp.zeros((ray_rows, 1), jnp.float32)] * 3
    for s in range(SEGS - 1, -1, -1):
        grad_trans = prefix[s] * sum(behind[c] * residual[c] for c in range(3))
        rows = pl.ds(s * ray_rows, ray_rows)
        mine = here[s * ray_rows : (s + 1) * ray_rows]
        which = entry_col[s * ray_rows : (s + 1) * ray_rows] // 4
        block = jnp.zeros((ray_rows, 128), jnp.float32)
        for ch in range(4):
            value = prefix[s] * residual[ch] if ch < 3 else grad_trans * seg(3, s)
            block = jnp.where(mine & (which == ch), value, block)
        per_entry[rows, :] = block
        behind = [seg(c, s) + seg(3, s) * behind[c] for c in range(3)]
    spread = exact_dot(place, per_entry[...])
    wide = []
    for ch in range(4):
        to_lanes = iota((128, LANES), 0) == 4 * ch + iota((128, LANES), 1) // SAMPLES
        wide.append(exact_dot(spread, to_lanes.astype(jnp.float32)))
    shading = sum(colour[c] * wide[c] for c in range(3))
    after = exact_dot(weight * shading, beyond)
    ups[0] = (shading * leaving - after - wide[3]) * steps * logistic(raw)
    for c in range(3):
        ups[1 + c] = weight * wide[c] * colour[c] * (1.0 - colour[c])

    row8 = iota((8, LANES), 0)

    def backward(g):
        b = brick_list[0, g]
        up8 = jnp.zeros((8, LANES), jnp.float32)
        for ch in range(4):
            line = jnp.broadcast_to(ups[ch, pl.ds(g, 1), :], (8, LANES))
            up8 = jnp.where(row8 == 4 + ch, line, up8)
        up = jnp.concatenate([jnp.zeros((ROWS - 8, LANES), jnp.float32), up8], axis=0)
        up = up.astype(jnp.bfloat16)
        grad_hidden = jnp.dot(weight_t[b], up, preferred_element_type=jnp.float32)
        grad_before = (grad_hidden * slope[g].astype(jnp.float32)).astype(jnp.bfloat16)
        dims = (((1,), (1,)), ((), ()))
        return lax.dot_general(
            encoded[g], grad_before, dims, preferred_element_type=jnp.float32
        ) + lax.dot_general(up, hidden[g], dims, preferred_element_type=jnp.float32)

    @pl.loop(0, turns)
    def _(turn):
        terms = [backward(together * turn + i) for i in range(together)]
        for i in range(together):
            grads[brick_list[0, together * turn + i]] += terms[i]


def own_rays(gathered, encoded, steps, group_row, group_col, place_col, brick_of, target):
    bricks = gathered.shape[0]
    ray_rows = target.shape[1]
    entries = ray_rows * SEGS
    groups = encoded.shape[0]
    vmem = pl.BlockSpec(memory_space=pltpu.VMEM)
    samples = groups * LANES
    return pl.pallas_call(
        functools.partial(rays_kernel, groups, bricks, ray_rows),
        out_shape=(
            jax.ShapeDtypeStruct((3, ray_rows), jnp.float32),
            jax.ShapeDtypeStruct((bricks, ROWS, HID), jnp.float32),
        ),
        in_specs=[pl.BlockSpec(memory_space=pltpu.SMEM)] + [vmem] * 7,
        out_specs=(vmem, vmem),
        scratch_shapes=[
            pltpu.VMEM((bricks, HID, ROWS), jnp.bfloat16),
            pltpu.VMEM((groups, HID, LANES), jnp.bfloat16),
            pltpu.VMEM((groups, HID, LANES), jnp.bfloat16),
            pltpu.VMEM((4, groups, LANES), jnp.float32),
            pltpu.VMEM((4, groups, LANES), jnp.float32),
            pltpu.VMEM((entries, 128), jnp.float32),
        ],
        compiler_params=pltpu.CompilerParams(vmem_limit_bytes=VMEM_BYTES),
        cost_estimate=pl.CostEstimate(
            flops=samples * HID * ROWS * 10,
            transcendentals=samples * HID,
            bytes_accessed=2 * bricks * ROWS * HID * 4,
        ),
        name="own_rays",
    )(brick_of, gathered, encoded, steps, group_row, group_col, place_col, target)


def partners(sizes):
    here = tuple(lax.axis_index(name) for name in AXES)

    def shifted(axis, step):
        place = list(here)
        place[axis] = lax.rem(here[axis] + step, sizes[axis])
        return tuple(place)

    others = [shifted(axis, step) for axis in range(3) for step in range(1, sizes[axis])]
    return here, shifted, others


def greet(others):
    barrier = pltpu.get_barrier_semaphore()
    for other in others:
        pl.semaphore_signal(barrier, inc=1, device_id=other, device_id_type=pl.DeviceIdType.MESH)
    pl.semaphore_wait(barrier, len(others))


def transfer(source, landing, send_sem, recv_sem, device):
    return pltpu.make_async_remote_copy(
        src_ref=source,
        dst_ref=landing,
        send_sem=send_sem,
        recv_sem=recv_sem,
        device_id=device,
        device_id_type=pl.DeviceIdType.MESH,
    )


def gather_kernel(
    sizes,
    groups,
    own,
    positions,
    spacing,
    crossings,
    out,
    encoded,
    steps,
    group_row,
    group_col,
    place_col,
    brick_of,
    points,
    sends,
    recvs,
):
    nx, ny, nz = sizes

    def encode_groups(first, end):
        @pl.loop(first, end)
        def _(turn):
            for g in (2 * turn, 2 * turn + 1):
                encoded[g] = encode_block(*[points[c, pl.ds(g, 1), :] for c in range(3)])

    (x, y, z), shifted, others = partners(sizes)
    greet(others)
    out[x, y, z] = own[...]
    started = []

    def block(dx, dy, dz):
        return out.at[
            lax.rem(x - dx + nx, nx), lax.rem(y - dy + ny, ny), lax.rem(z - dz + nz, nz)
        ]

    def send(source, axis, step, came):
        where = (came[0] * ny + came[1]) * nz + came[2]
        copy = transfer(source, source, sends.at[where], recvs.at[where], shifted(axis, step))
        copy.start()
        started.append(copy)

    def arrive(came):
        where = (came[0] * ny + came[1]) * nz + came[2]
        landed = block(*came)
        transfer(landed, landed, sends.at[where], recvs.at[where], others[0]).wait_recv()

    for dx in range(1, nx):
        send(block(0, 0, 0), 0, dx, (dx, 0, 0))
    number_groups(nx * ny * nz, crossings, group_row, group_col, place_col, brick_of)
    for dx in range(nx):
        if dx > 0:
            arrive((dx, 0, 0))
        for dy in range(1, ny):
            send(block(dx, 0, 0), 1, dy, (dx, dy, 0))
        for dz in range(1, nz):
            send(block(dx, 0, 0), 2, dz, (dx, 0, dz))
    place_points(groups, positions, spacing, group_row, place_col, points, steps)
    turns = groups // 2
    for dx in range(nx):
        encode_groups(turns * dx // nx, turns * (dx + 1) // nx)
        for dy in range(1, ny):
            arrive((dx, dy, 0))
            for dz in range(1, nz):
                send(block(dx, dy, 0), 2, dz, (dx, dy, dz))
    for dx in range(nx):
        for dy in range(ny):
            for dz in range(1, nz):
                arrive((dx, dy, dz))
    for copy in started:
        copy.wait_send()


def gather_weights(packed, positions, spacing, crossings, sizes):
    count = sizes[0] * sizes[1] * sizes[2]
    ray_rows = crossings.shape[0]
    entries = ray_rows * SEGS
    groups = -(-((entries + (PACK - 1) * count) // PACK) // 8) * 8
    listed = -(-(groups + 1) // 128) * 128
    vmem = pl.BlockSpec(memory_space=pltpu.VMEM)
    gathered, *rest = pl.pallas_call(
        functools.partial(gather_kernel, sizes, groups),
        out_shape=(
            jax.ShapeDtypeStruct(sizes + packed.shape, jnp.float32),
            jax.ShapeDtypeStruct((groups, ROWS, LANES), jnp.bfloat16),
            jax.ShapeDtypeStruct((groups, LANES), jnp.float32),
            jax.ShapeDtypeStruct((1, entries), jnp.int32),
            jax.ShapeDtypeStruct((entries, 1), jnp.int32),
            jax.ShapeDtypeStruct((entries, 1), jnp.int32),
            jax.ShapeDtypeStruct((1, listed), jnp.int32),
        ),
        in_specs=[vmem] * 4,
        out_specs=[vmem] * 7,
        scratch_shapes=[
            pltpu.VMEM((3, groups, LANES), jnp.float32),
            pltpu.SemaphoreType.DMA((count,)),
            pltpu.SemaphoreType.DMA((count,)),
        ],
        compiler_params=pltpu.CompilerParams(
            collective_id=0, has_side_effects=True, vmem_limit_bytes=VMEM_BYTES
        ),
        name="gather_weights",
    )(packed, positions, spacing.T, crossings.T)
    return gathered.reshape((count,) + packed.shape), rest


def update_kernel(
    sizes, grads, out_first, out_head, from_z, sum_z, from_y, sum_y, from_x, parts, sends, recvs, small_s, small_r
):
    nx, ny, nz = sizes
    (x, y, z), shifted, others = partners(sizes)
    greet(others)
    started = []

    def place(step, axis):
        return lax.rem((x, y, z)[axis] + step, sizes[axis])

    def number(step):
        return (step[0] * ny + step[1]) * nz + step[2]

    def send(source, landing, where, axis, step):
        copy = transfer(source, landing, sends.at[where], recvs.at[where], shifted(axis, step))
        copy.start()
        started.append(copy)

    def arrive(landing, where):
        transfer(landing, landing, sends.at[where], recvs.at[where], others[0]).wait_recv()

    order_x = list(range(1, nx)) + [0]
    order_y = list(range(1, ny)) + [0]
    for dx in order_x:
        for dy in order_y:
            for dz in range(1, nz):
                send(
                    grads.at[place(dx, 0), place(dy, 1), place(dz, 2)],
                    from_z.at[dx, dy, dz - 1],
                    number((dx, dy, dz)),
                    2,
                    dz,
                )
    for dx in order_x:
        for dy in order_y:
            total = grads[place(dx, 0), place(dy, 1), z]
            for dz in range(1, nz):
                arrive(from_z.at[dx, dy, dz - 1], number((dx, dy, dz)))
                total = total + from_z[dx, dy, dz - 1]
            sum_z[dx, dy] = total
            if dy > 0:
                send(sum_z.at[dx, dy], from_y.at[dx, dy - 1], number((dx, dy, 0)), 1, dy)
    for dx in order_x:
        total = sum_z[dx, 0]
        for dy in range(1, ny):
            arrive(from_y.at[dx, dy - 1], number((dx, dy, 0)))
            total = total + from_y[dx, dy - 1]
        sum_y[dx] = total
        if dx > 0:
            send(sum_y.at[dx], from_x.at[dx - 1], number((dx, 0, 0)), 0, dx)
    for dx in range(1, nx):
        arrive(from_x.at[dx - 1], number((dx, 0, 0)))
        total = total + from_x[dx - 1]
    square = total * total
    part = jnp.zeros((8, 128), jnp.float32)
    for i in range(0, square.shape[0], 8):
        for j in range(0, square.shape[1], 128):
            part = part + square[i : i + 8, j : j + 128]
    slot = 0
    for axis in range(3):
        parts[slot] = part
        copies = []
        for step in range(1, sizes[axis]):
            copy = transfer(
                parts.at[slot],
                parts.at[slot + step],
                small_s.at[slot + step],
                small_r.at[slot + step],
                shifted(axis, step),
            )
            copy.start()
            copies.append(copy)
        for step in range(1, sizes[axis]):
            copies[step - 1].wait_recv()
            part = part + parts[slot + step]
        started.extend(copies)
        slot += sizes[axis]
    overall = jnp.sum(part, keepdims=True)
    count_all = nx * ny * nz * total.size
    scaled = total * lax.rsqrt(overall / count_all + NORM_EPS)
    out_first[...] = scaled[:ENC]
    out_head[...] = scaled[ENC:]
    for copy in started:
        copy.wait_send()


def sum_and_scale(grads, sizes):
    nx, ny, nz = sizes
    count = nx * ny * nz
    tile = grads.shape[1:]
    vmem = pl.BlockSpec(memory_space=pltpu.VMEM)
    small = nx + ny + nz
    return pl.pallas_call(
        functools.partial(update_kernel, sizes),
        out_shape=(
            jax.ShapeDtypeStruct((ENC, tile[1]), jnp.float32),
            jax.ShapeDtypeStruct((tile[0] - ENC, tile[1]), jnp.float32),
        ),
        in_specs=[vmem],
        out_specs=(vmem, vmem),
        scratch_shapes=[
            pltpu.VMEM((nx, ny, max(nz - 1, 1)) + tile, jnp.float32),
            pltpu.VMEM((nx, ny) + tile, jnp.float32),
            pltpu.VMEM((nx, max(ny - 1, 1)) + tile, jnp.float32),
            pltpu.VMEM((nx,) + tile, jnp.float32),
            pltpu.VMEM((max(nx - 1, 1),) + tile, jnp.float32),
            pltpu.VMEM((small, 8, 128), jnp.float32),
            pltpu.SemaphoreType.DMA((count,)),
            pltpu.SemaphoreType.DMA((count,)),
            pltpu.SemaphoreType.DMA((small,)),
            pltpu.SemaphoreType.DMA((small,)),
        ],
        compiler_params=pltpu.CompilerParams(
            collective_id=1, has_side_effects=True, vmem_limit_bytes=VMEM_BYTES
        ),
        name="sum_and_scale",
    )(grads.reshape(sizes + tile))


def by_gather(positions, spacing, crossings, target, first_weight, head_weight):
    sizes = tuple(lax.axis_size(name) for name in AXES)
    packed = jnp.concatenate(
        [first_weight[0].astype(jnp.float32).T, head_weight[0].astype(jnp.float32)], axis=0
    )
    gathered, rest = gather_weights(packed, positions, spacing, crossings, sizes)
    rendered, grads = own_rays(gathered, *rest, target)
    first, head = sum_and_scale(grads, sizes)
    return (rendered, first.T[None], head[None])


def encode(points):
    scales = 2.0 ** jnp.arange(FREQS, dtype=jnp.float32) * PI_VALUE
    angles = scales[:, None, None] * points[None]
    wave_table = jnp.stack([jnp.sin(angles), jnp.cos(angles)], axis=1)
    return wave_table.reshape(6 * FREQS, points.shape[1]).astype(jnp.bfloat16)


def network(first_local, head_local, points):
    encoded = encode(points)
    before = jnp.dot(first_local, encoded, preferred_element_type=jnp.float32)
    hidden = jax.nn.silu(before).astype(jnp.bfloat16)
    output = jnp.dot(head_local, hidden, preferred_element_type=jnp.float32)
    return (encoded, before, hidden, output)


def activate(output):
    return (jax.nn.softplus(output[0]), jax.nn.sigmoid(output[1:]))


def segment_forward(density, colour, step_len):
    optical = density * step_len[:, None]
    inclusive = jnp.cumsum(optical, axis=1)
    leaving = jnp.exp(-inclusive)
    weight = jnp.exp(optical - inclusive) - leaving
    seg_colour = jnp.sum(weight[None] * colour, axis=2)
    return (seg_colour, leaving[:, -1], weight, leaving)


def segment_backward(colour, weight, leaving, step_len, grad_colour, grad_trans):
    shading = jnp.sum(colour * grad_colour[:, :, None], axis=0)
    weighted = weight * shading
    after = jnp.sum(weighted, axis=1, keepdims=True) - jnp.cumsum(weighted, axis=1)
    grad_depth = shading * leaving - after - (grad_trans * leaving[:, -1])[:, None]
    grad_density = grad_depth * step_len[:, None]
    grad_sample = weight[None] * grad_colour[:, :, None]
    return (grad_density, grad_sample)


def ray_level(seg_colour, seg_trans, target):
    seg_total = seg_trans.shape[1]
    through = jnp.cumprod(seg_trans, axis=1)
    prefix = jnp.concatenate([jnp.ones_like(seg_trans[:, :1]), through[:, :-1]], axis=1)
    rendered = jnp.sum(prefix[None] * seg_colour, axis=2)
    residual = rendered - target
    grad_colour = prefix[None] * residual[:, :, None]
    behind_list = [jnp.zeros_like(rendered)]
    for offset in range(seg_total - 1, 0, -1):
        behind_list.append(seg_colour[:, :, offset] + seg_trans[:, offset][None] * behind_list[-1])
    behind = jnp.stack(behind_list[::-1], axis=2)
    grad_trans = prefix * jnp.sum(behind * residual[:, :, None], axis=0)
    return (rendered, grad_colour, grad_trans)


def output_grad(output, grad_density, grad_sample):
    colour = jax.nn.sigmoid(output[1:])
    first_row = grad_density * jax.nn.sigmoid(output[0])
    others = grad_sample * colour * (1.0 - colour)
    return jnp.concatenate([first_row[None], others], axis=0).astype(jnp.bfloat16)


def network_grad(head_local, encoded, before, hidden, upstream):
    grad_head = lax.dot_general(
        upstream, hidden, (((1,), (1,)), ((), ())), preferred_element_type=jnp.float32
    )
    grad_hidden = lax.dot_general(
        head_local, upstream, (((0,), (0,)), ((), ())), preferred_element_type=jnp.float32
    )
    logistic = jax.nn.sigmoid(before)
    grad_before = (grad_hidden * logistic * (1.0 + before * (1.0 - logistic))).astype(jnp.bfloat16)
    grad_first = lax.dot_general(
        grad_before, encoded, (((1,), (1,)), ((), ())), preferred_element_type=jnp.float32
    )
    return (grad_first, grad_head)


def by_exchange(positions, spacing, crossings, target, first_weight, head_weight):
    across = lax.axis_size(("gx", "gy"))
    along_count = lax.axis_size("gz")
    devices = across * along_count
    ray_rows = crossings.shape[0]
    entries = ray_rows * SEGS
    capacity = 2 * entries // devices
    total_slots = devices * capacity
    sample_total = total_slots * SAMPLES
    block_size = math.gcd(sample_total, BLOCK_LIMIT)
    block_count = sample_total // block_size
    block_segs = block_size // SAMPLES
    first_local = first_weight[0]
    head_local = head_weight[0]
    brick_ids = crossings.reshape(entries)
    order_rank = jnp.arange(entries, dtype=jnp.int32)
    earlier = (brick_ids[:, None] == brick_ids[None, :]) & (
        order_rank[None, :] < order_rank[:, None]
    )
    column = brick_ids * capacity + jnp.sum(earlier.astype(jnp.int32), axis=1)
    own_points = positions.reshape(3, entries, SAMPLES)
    own_steps = spacing.reshape(entries)
    send_points = jnp.zeros((3, total_slots, SAMPLES), jnp.float32).at[:, column, :].set(own_points)
    send_steps = jnp.zeros((1, total_slots), jnp.float32).at[0, column].set(own_steps)
    got_points, got_steps = (
        lax.all_to_all(
            lax.all_to_all(
                send_points.reshape(3, across, along_count, capacity * SAMPLES),
                ("gx", "gy"),
                split_axis=1,
                concat_axis=1,
                tiled=True,
            ),
            "gz",
            split_axis=2,
            concat_axis=2,
            tiled=True,
        ),
        lax.all_to_all(
            lax.all_to_all(
                send_steps.reshape(1, across, along_count, capacity),
                ("gx", "gy"),
                split_axis=1,
                concat_axis=1,
                tiled=True,
            ),
            "gz",
            split_axis=2,
            concat_axis=2,
            tiled=True,
        ),
    )
    point_blocks = got_points.reshape(3, block_count, block_size).transpose(1, 0, 2)
    step_blocks = got_steps.reshape(block_count, block_segs)

    def forward_turn(unused, inputs):
        block_points, block_steps = inputs
        encoded, before, hidden, output = network(first_local, head_local, block_points)
        density, colour = activate(output)
        result = jnp.concatenate([density[None], colour], axis=0)
        return (unused, result)

    unused, results = lax.scan(
        forward_turn, jnp.zeros((), jnp.float32), (point_blocks, step_blocks)
    )
    values = results.transpose(1, 0, 2).reshape(4, across, along_count, capacity * SAMPLES)
    returned = lax.all_to_all(
        lax.all_to_all(values, ("gx", "gy"), split_axis=1, concat_axis=1, tiled=True),
        "gz",
        split_axis=2,
        concat_axis=2,
        tiled=True,
    )
    owned = returned.reshape(4, total_slots, SAMPLES)[:, column, :]
    seg_colour, seg_trans, weight, leaving = segment_forward(owned[0], owned[1:], own_steps)
    rendered, grad_colour, grad_trans = ray_level(
        seg_colour.reshape(3, ray_rows, SEGS), seg_trans.reshape(ray_rows, SEGS), target
    )
    grad_density, grad_sample = segment_backward(
        owned[1:],
        weight,
        leaving,
        own_steps,
        grad_colour.reshape(3, entries),
        grad_trans.reshape(entries),
    )
    stacked = jnp.concatenate([grad_density[None], grad_sample], axis=0)
    send_grads = jnp.zeros((4, total_slots, SAMPLES), jnp.float32).at[:, column, :].set(stacked)
    got_grads = lax.all_to_all(
        lax.all_to_all(
            send_grads.reshape(4, across, along_count, capacity * SAMPLES),
            ("gx", "gy"),
            split_axis=1,
            concat_axis=1,
            tiled=True,
        ),
        "gz",
        split_axis=2,
        concat_axis=2,
        tiled=True,
    )
    grad_blocks = got_grads.reshape(4, block_count, block_size).transpose(1, 0, 2)

    def backward_turn(totals, inputs):
        block_points, block_steps, block_upstream = inputs
        encoded, before, hidden, output = network(first_local, head_local, block_points)
        grad_density = block_upstream[0]
        grad_sample = block_upstream[1:]
        upstream = output_grad(output, grad_density, grad_sample)
        grad_first, grad_head = network_grad(head_local, encoded, before, hidden, upstream)
        return ((totals[0] + grad_first, totals[1] + grad_head), None)

    start_totals = (
        jnp.zeros(first_local.shape, jnp.float32),
        jnp.zeros(head_local.shape, jnp.float32),
    )
    totals, unused_out = lax.scan(
        backward_turn, start_totals, (point_blocks, step_blocks, grad_blocks)
    )
    grad_first, grad_head = totals
    square_sum = jnp.sum(grad_first * grad_first) + jnp.sum(grad_head * grad_head)
    overall = lax.psum(square_sum, ("gx", "gy", "gz"))
    count_all = devices * (grad_first.size + grad_head.size)
    scale = lax.rsqrt(overall / count_all + NORM_EPS)
    return (rendered, (grad_first * scale)[None], (grad_head * scale)[None])


def solution(mesh):
    in_specs = (
        P(None, ("gx", "gy", "gz"), None),
        P(("gx", "gy", "gz"), None),
        P(("gx", "gy", "gz"), None),
        P(None, ("gx", "gy", "gz")),
        P(("gx", "gy", "gz"), None, None),
        P(("gx", "gy", "gz"), None, None),
    )
    out_specs = (
        P(None, ("gx", "gy", "gz")),
        P(("gx", "gy", "gz"), None, None),
        P(("gx", "gy", "gz"), None, None),
    )
    body = by_gather if mesh.size <= GATHER_LIMIT else by_exchange
    return jax.shard_map(
        body, mesh=mesh, in_specs=in_specs, out_specs=out_specs, check_vma=False
    )
```

```python
import functools
import math

import jax
import jax.numpy as jnp
from jax import lax
from jax.experimental import pallas as pl
from jax.experimental.pallas import tpu as pltpu
from jax.sharding import PartitionSpec as P

FREQS = 10
SAMPLES = 64
SEGS = 8
AXES = ("gx", "gy", "gz")
ENC = 6 * FREQS
ROWS = ENC + 4
HID = 256
PACK = 4
LANES = PACK * SAMPLES
GATHER_LIMIT = 64
VMEM_BYTES = 58 * 1024 * 1024
HIGHEST = lax.Precision.HIGHEST


PI_VALUE = 3.141592653589793
NORM_EPS = 1e-06
BLOCK_LIMIT = 2048


def exact_dot(a, b):
    return jnp.dot(a, b, precision=HIGHEST, preferred_element_type=jnp.float32)


def iota(shape, dim):
    return lax.broadcasted_iota(jnp.int32, shape, dim)


def logistic(x):
    return 0.5 + 0.5 * jnp.tanh(0.5 * x)


def encode_block(p0, p1, p2):
    shape = (ROWS, LANES)
    row = iota((ROWS, 1), 0)
    freq = row // 6
    axis = row % 3
    scale = jnp.zeros((ROWS, 1), jnp.float32)
    for k in range(FREQS):
        scale = jnp.where(freq == k, 2.0 ** (k - 1), scale)
    is_cos = (row % 6 // 3 == 1) & (row < ENC)
    shift = jnp.where(is_cos, 0.0, 0.25)
    point = jnp.where(
        axis == 0,
        jnp.broadcast_to(p0, shape),
        jnp.where(axis == 1, jnp.broadcast_to(p1, shape), jnp.broadcast_to(p2, shape)),
    )
    turns = point * scale - shift
    arg = 0.25 - jnp.abs(turns - jnp.round(turns))
    square = arg * arg
    circle = 2.0 * PI_VALUE
    total = jnp.full(shape, -(circle**11) / math.factorial(11), jnp.float32)
    for power in (9, 7, 5, 3, 1):
        factor = circle**power / math.factorial(power)
        total = total * square + (factor if power % 4 == 1 else -factor)
    return (total * arg).astype(jnp.bfloat16)


def to_column(row):
    n = row.shape[1]
    return jnp.sum(jnp.where(iota((n, n), 0) == iota((n, n), 1), row, 0.0), axis=1, keepdims=True)


def to_row(column):
    n = column.shape[0]
    return jnp.sum(
        jnp.where(iota((n, n), 0) == iota((n, n), 1), column, 0.0), axis=0, keepdims=True
    )


def number_groups(bricks, crossings, group_row, group_col, place_col, brick_of):
    ids_col = jnp.concatenate(
        [to_column(crossings[s : s + 1, :].astype(jnp.float32)) for s in range(SEGS)], axis=0
    )
    entries = ids_col.shape[0]
    ids_row = to_row(ids_col)
    square = (entries, entries)
    same = ids_col == ids_row
    rank_col = jnp.sum(
        jnp.where(same & (iota(square, 1) < iota(square, 0)), 1.0, 0.0), axis=1, keepdims=True
    )
    rank_row = jnp.sum(
        jnp.where(same & (iota(square, 0) < iota(square, 1)), 1.0, 0.0), axis=0, keepdims=True
    )
    wide = 128
    of_brick = ids_col == iota((entries, wide), 1).astype(jnp.float32)
    counts = jnp.sum(jnp.where(of_brick, 1.0, 0.0), axis=0, keepdims=True)
    needed_row = jnp.floor((counts + (PACK - 1)) * (1.0 / PACK))
    needed_col = to_column(needed_row)
    pair = (wide, wide)
    start_row = jnp.sum(
        jnp.where(iota(pair, 0) < iota(pair, 1), needed_col, 0.0), axis=0, keepdims=True
    )
    start_col = to_column(start_row)
    first_col = jnp.sum(jnp.where(of_brick, start_row, 0.0), axis=1, keepdims=True)
    of_brick_t = ids_row == iota((wide, entries), 0).astype(jnp.float32)
    first_row = jnp.sum(jnp.where(of_brick_t, start_col, 0.0), axis=0, keepdims=True)
    full_col = jnp.floor(rank_col * (1.0 / PACK))
    full_row = jnp.floor(rank_row * (1.0 / PACK))
    group_col[...] = (first_col + full_col).astype(jnp.int32)
    group_row[...] = (first_row + full_row).astype(jnp.int32)
    place_col[...] = (rank_col - PACK * full_col).astype(jnp.int32)
    shape = (wide, brick_of.shape[1])
    number = iota(shape, 1).astype(jnp.float32)
    passed = (start_col + needed_col <= number) & (iota(shape, 0) < bricks)
    found = jnp.sum(jnp.where(passed, 1.0, 0.0), axis=0, keepdims=True)
    total = jnp.sum(needed_row, axis=1, keepdims=True)
    last = iota(brick_of.shape, 1) == brick_of.shape[1] - 1
    brick_of[...] = jnp.where(last, total, jnp.minimum(found, bricks - 1.0)).astype(jnp.int32)


def place_points(groups, positions, spacing, group_row, place_col, points, steps):
    ray_rows = positions.shape[1]
    entries = ray_rows * SEGS
    place = (iota((groups, entries), 0) == group_row[...]).astype(jnp.float32)
    chosen = place_col[...] == iota((entries, LANES), 1) // SAMPLES
    low = iota((ray_rows, 2 * SAMPLES), 1) < SAMPLES
    for c in range(3):
        parts = []
        for pair in range(SEGS // 2):
            both = positions[c, :, 2 * SAMPLES * pair : 2 * SAMPLES * (pair + 1)]
            turned = pltpu.roll(both, SAMPLES, 1)
            for half in (jnp.where(low, both, turned), jnp.where(low, turned, both)):
                parts.append(jnp.concatenate([half] * (LANES // (2 * SAMPLES)), axis=1))
        values = jnp.where(chosen, jnp.concatenate(parts, axis=0), 0.0)
        points[c] = exact_dot(place, values)
    lengths = jnp.concatenate(
        [to_column(spacing[s : s + 1, :]) for s in range(SEGS)], axis=0
    )
    steps[...] = exact_dot(place, jnp.where(chosen, lengths, 0.0))


def rays_kernel(
    groups,
    bricks,
    ray_rows,
    brick_list,
    weights,
    encoded,
    steps_in,
    group_row,
    group_col,
    place_col,
    target,
    rendered_out,
    grads,
    weight_t,
    grads_t,
    hidden,
    slope,
    outs,
    ups,
    per_entry,
):
    entries = ray_rows * SEGS
    together = 4
    turns = (brick_list[0, brick_list.shape[1] - 1] + together - 1) // together
    place = (iota((groups, entries), 0) == group_row[...]).astype(jnp.float32)
    outs[...] = jnp.zeros_like(outs)
    grads_t[...] = jnp.zeros_like(grads_t)

    few = math.gcd(bricks, 4)

    @pl.loop(0, bricks // few)
    def _(turn):
        for i in range(few):
            weight_t[few * turn + i] = (0.5 * weights[few * turn + i].T).astype(jnp.bfloat16)

    def forward(g):
        b = brick_list[0, g]
        half = jnp.dot(weight_t[b], encoded[g], preferred_element_type=jnp.float32)
        bent = jnp.tanh(half)
        act = half + half * bent
        slope[g] = ((1.0 + act) + bent * (1.0 - act)).astype(jnp.bfloat16)
        hid = act.astype(jnp.bfloat16)
        hidden[g] = hid
        head = weights[b, ROWS - 8 :, :].astype(jnp.bfloat16)
        out = jnp.dot(head, hid, preferred_element_type=jnp.float32)
        for ch in range(4):
            outs[ch, pl.ds(g, 1), :] = out[4 + ch : 5 + ch, :]

    @pl.loop(0, turns)
    def _(turn):
        for i in range(together):
            forward(together * turn + i)

    same = iota((LANES, LANES), 0) // SAMPLES == iota((LANES, LANES), 1) // SAMPLES
    upto = (same & (iota((LANES, LANES), 0) <= iota((LANES, LANES), 1))).astype(jnp.float32)
    beyond = (same & (iota((LANES, LANES), 0) > iota((LANES, LANES), 1))).astype(jnp.float32)
    steps = steps_in[...]
    raw = outs[0]
    density = jnp.maximum(raw, 0.0) + jnp.log1p(jnp.exp(-jnp.abs(raw)))
    colour = [logistic(outs[1 + c]) for c in range(3)]
    optical = density * steps
    inclusive = exact_dot(optical, upto)
    leaving = jnp.exp(-inclusive)
    weight = jnp.exp(optical - inclusive) - leaving
    lane = iota((LANES, 128), 0)
    col = iota((LANES, 128), 1)
    sums = jnp.zeros((groups, 128), jnp.float32)
    for ch in range(4):
        pick = col == 4 * ch + lane // SAMPLES
        if ch == 3:
            pick = pick & (lane % SAMPLES == SAMPLES - 1)
        sums = sums + exact_dot(weight * colour[ch] if ch < 3 else leaving, pick.astype(jnp.float32))
    back = (iota((entries, groups), 1) == group_col[...]).astype(jnp.float32)
    found = exact_dot(back, sums)
    entry_col = iota((entries, 128), 1)
    here = entry_col % 4 == place_col[...]
    values = [
        jnp.sum(jnp.where(here & (entry_col // 4 == ch), found, 0.0), axis=1, keepdims=True)
        for ch in range(4)
    ]

    def seg(ch, s):
        return values[ch][s * ray_rows : (s + 1) * ray_rows]

    prefix = [jnp.ones((ray_rows, 1), jnp.float32)]
    for s in range(SEGS - 1):
        prefix.append(prefix[s] * seg(3, s))
    residual = []
    for c in range(3):
        shown = sum(prefix[s] * seg(c, s) for s in range(SEGS))
        rendered_out[c : c + 1, :] = to_row(shown)
        residual.append(shown - to_column(target[c : c + 1, :]))
    behind = [jnp.zeros((ray_rows, 1), jnp.float32)] * 3
    for s in range(SEGS - 1, -1, -1):
        grad_trans = prefix[s] * sum(behind[c] * residual[c] for c in range(3))
        rows = pl.ds(s * ray_rows, ray_rows)
        mine = here[s * ray_rows : (s + 1) * ray_rows]
        which = entry_col[s * ray_rows : (s + 1) * ray_rows] // 4
        block = jnp.zeros((ray_rows, 128), jnp.float32)
        for ch in range(4):
            value = prefix[s] * residual[ch] if ch < 3 else grad_trans * seg(3, s)
            block = jnp.where(mine & (which == ch), value, block)
        per_entry[rows, :] = block
        behind = [seg(c, s) + seg(3, s) * behind[c] for c in range(3)]
    spread = exact_dot(place, per_entry[...])
    wide = []
    for ch in range(4):
        to_lanes = iota((128, LANES), 0) == 4 * ch + iota((128, LANES), 1) // SAMPLES
        wide.append(exact_dot(spread, to_lanes.astype(jnp.float32)))
    shading = sum(colour[c] * wide[c] for c in range(3))
    after = exact_dot(weight * shading, beyond)
    ups[0] = (shading * leaving - after - wide[3]) * steps * logistic(raw)
    for c in range(3):
        ups[1 + c] = weight * wide[c] * colour[c] * (1.0 - colour[c])

    row8 = iota((8, LANES), 0)

    def backward(g):
        b = brick_list[0, g]
        up8 = jnp.zeros((8, LANES), jnp.float32)
        for ch in range(4):
            line = jnp.broadcast_to(ups[ch, pl.ds(g, 1), :], (8, LANES))
            up8 = jnp.where(row8 == 4 + ch, line, up8)
        up = jnp.concatenate([jnp.zeros((ROWS - 8, LANES), jnp.float32), up8], axis=0)
        up = up.astype(jnp.bfloat16)
        grad_hidden = jnp.dot(weight_t[b], up, preferred_element_type=jnp.float32)
        grad_before = (grad_hidden * slope[g].astype(jnp.float32)).astype(jnp.bfloat16)
        dims = (((1,), (1,)), ((), ()))
        return lax.dot_general(
            grad_before, encoded[g], dims, preferred_element_type=jnp.float32
        ) + lax.dot_general(hidden[g], up, dims, preferred_element_type=jnp.float32)

    @pl.loop(0, turns)
    def _(turn):
        terms = [backward(together * turn + i) for i in range(together)]
        for i in range(together):
            grads_t[brick_list[0, together * turn + i]] += terms[i]

    @pl.loop(0, bricks // few)
    def _(turn):
        for i in range(few):
            grads[few * turn + i] = grads_t[few * turn + i].T


def own_rays(gathered, encoded, steps, group_row, group_col, place_col, brick_of, target):
    bricks = gathered.shape[0]
    ray_rows = target.shape[1]
    entries = ray_rows * SEGS
    groups = encoded.shape[0]
    vmem = pl.BlockSpec(memory_space=pltpu.VMEM)
    samples = groups * LANES
    return pl.pallas_call(
        functools.partial(rays_kernel, groups, bricks, ray_rows),
        out_shape=(
            jax.ShapeDtypeStruct((3, ray_rows), jnp.float32),
            jax.ShapeDtypeStruct((bricks, ROWS, HID), jnp.float32),
        ),
        in_specs=[pl.BlockSpec(memory_space=pltpu.SMEM)] + [vmem] * 7,
        out_specs=(vmem, vmem),
        scratch_shapes=[
            pltpu.VMEM((bricks, HID, ROWS), jnp.bfloat16),
            pltpu.VMEM((bricks, HID, ROWS), jnp.float32),
            pltpu.VMEM((groups, HID, LANES), jnp.bfloat16),
            pltpu.VMEM((groups, HID, LANES), jnp.bfloat16),
            pltpu.VMEM((4, groups, LANES), jnp.float32),
            pltpu.VMEM((4, groups, LANES), jnp.float32),
            pltpu.VMEM((entries, 128), jnp.float32),
        ],
        compiler_params=pltpu.CompilerParams(vmem_limit_bytes=VMEM_BYTES),
        cost_estimate=pl.CostEstimate(
            flops=samples * HID * ROWS * 10,
            transcendentals=samples * HID,
            bytes_accessed=2 * bricks * ROWS * HID * 4,
        ),
        name="own_rays",
    )(brick_of, gathered, encoded, steps, group_row, group_col, place_col, target)


def partners(sizes):
    here = tuple(lax.axis_index(name) for name in AXES)

    def shifted(axis, step):
        place = list(here)
        place[axis] = lax.rem(here[axis] + step, sizes[axis])
        return tuple(place)

    others = [shifted(axis, step) for axis in range(3) for step in range(1, sizes[axis])]
    return here, shifted, others


def greet(others):
    barrier = pltpu.get_barrier_semaphore()
    for other in others:
        pl.semaphore_signal(barrier, inc=1, device_id=other, device_id_type=pl.DeviceIdType.MESH)
    pl.semaphore_wait(barrier, len(others))


def transfer(source, landing, send_sem, recv_sem, device):
    return pltpu.make_async_remote_copy(
        src_ref=source,
        dst_ref=landing,
        send_sem=send_sem,
        recv_sem=recv_sem,
        device_id=device,
        device_id_type=pl.DeviceIdType.MESH,
    )


def gather_kernel(
    sizes,
    groups,
    own_first,
    own_head,
    positions,
    spacing,
    crossings,
    out,
    encoded,
    steps,
    group_row,
    group_col,
    place_col,
    brick_of,
    points,
    sends,
    recvs,
):
    nx, ny, nz = sizes

    def encode_groups(first, end):
        @pl.loop(first, end)
        def _(turn):
            for g in (2 * turn, 2 * turn + 1):
                encoded[g] = encode_block(*[points[c, pl.ds(g, 1), :] for c in range(3)])

    (x, y, z), shifted, others = partners(sizes)
    greet(others)
    out[x, y, z, :ENC, :] = own_first[...].astype(jnp.float32)
    out[x, y, z, ENC:, :] = own_head[...].astype(jnp.float32)
    started = []

    def block(dx, dy, dz):
        return out.at[
            lax.rem(x - dx + nx, nx), lax.rem(y - dy + ny, ny), lax.rem(z - dz + nz, nz)
        ]

    def send(source, axis, step, came):
        where = (came[0] * ny + came[1]) * nz + came[2]
        copy = transfer(source, source, sends.at[where], recvs.at[where], shifted(axis, step))
        copy.start()
        started.append(copy)

    def arrive(came):
        where = (came[0] * ny + came[1]) * nz + came[2]
        landed = block(*came)
        transfer(landed, landed, sends.at[where], recvs.at[where], others[0]).wait_recv()

    for dx in range(1, nx):
        send(block(0, 0, 0), 0, dx, (dx, 0, 0))
    number_groups(nx * ny * nz, crossings, group_row, group_col, place_col, brick_of)
    for dx in range(nx):
        if dx > 0:
            arrive((dx, 0, 0))
        for dy in range(1, ny):
            send(block(dx, 0, 0), 1, dy, (dx, dy, 0))
        for dz in range(1, nz):
            send(block(dx, 0, 0), 2, dz, (dx, 0, dz))
    place_points(groups, positions, spacing, group_row, place_col, points, steps)
    turns = groups // 2
    for dx in range(nx):
        encode_groups(turns * dx // nx, turns * (dx + 1) // nx)
        for dy in range(1, ny):
            arrive((dx, dy, 0))
            for dz in range(1, nz):
                send(block(dx, dy, 0), 2, dz, (dx, dy, dz))
    for dx in range(nx):
        for dy in range(ny):
            for dz in range(1, nz):
                arrive((dx, dy, dz))
    for copy in started:
        copy.wait_send()


def gather_weights(first, head, positions, spacing, crossings, sizes):
    count = sizes[0] * sizes[1] * sizes[2]
    ray_rows = crossings.shape[0]
    entries = ray_rows * SEGS
    groups = -(-((entries + (PACK - 1) * count) // PACK) // 8) * 8
    listed = -(-(groups + 1) // 128) * 128
    vmem = pl.BlockSpec(memory_space=pltpu.VMEM)
    gathered, *rest = pl.pallas_call(
        functools.partial(gather_kernel, sizes, groups),
        out_shape=(
            jax.ShapeDtypeStruct(sizes + (ROWS, HID), jnp.float32),
            jax.ShapeDtypeStruct((groups, ROWS, LANES), jnp.bfloat16),
            jax.ShapeDtypeStruct((groups, LANES), jnp.float32),
            jax.ShapeDtypeStruct((1, entries), jnp.int32),
            jax.ShapeDtypeStruct((entries, 1), jnp.int32),
            jax.ShapeDtypeStruct((entries, 1), jnp.int32),
            jax.ShapeDtypeStruct((1, listed), jnp.int32),
        ),
        in_specs=[vmem] * 5,
        out_specs=[vmem] * 7,
        scratch_shapes=[
            pltpu.VMEM((3, groups, LANES), jnp.float32),
            pltpu.SemaphoreType.DMA((count,)),
            pltpu.SemaphoreType.DMA((count,)),
        ],
        compiler_params=pltpu.CompilerParams(
            collective_id=0, has_side_effects=True, vmem_limit_bytes=VMEM_BYTES
        ),
        name="gather_weights",
    )(first, head, positions, spacing.T, crossings.T)
    return gathered.reshape((count, ROWS, HID)), rest


def update_kernel(
    sizes, grads, out_first, out_head, from_z, sum_z, from_y, sum_y, from_x, parts, sends, recvs, small_s, small_r
):
    nx, ny, nz = sizes
    (x, y, z), shifted, others = partners(sizes)
    greet(others)
    started = []

    def place(step, axis):
        return lax.rem((x, y, z)[axis] + step, sizes[axis])

    def number(step):
        return (step[0] * ny + step[1]) * nz + step[2]

    def send(source, landing, where, axis, step):
        copy = transfer(source, landing, sends.at[where], recvs.at[where], shifted(axis, step))
        copy.start()
        started.append(copy)

    def arrive(landing, where):
        transfer(landing, landing, sends.at[where], recvs.at[where], others[0]).wait_recv()

    order_x = list(range(1, nx)) + [0]
    order_y = list(range(1, ny)) + [0]
    for dx in order_x:
        for dy in order_y:
            for dz in range(1, nz):
                send(
                    grads.at[place(dx, 0), place(dy, 1), place(dz, 2)],
                    from_z.at[dx, dy, dz - 1],
                    number((dx, dy, dz)),
                    2,
                    dz,
                )
    for dx in order_x:
        for dy in order_y:
            total = grads[place(dx, 0), place(dy, 1), z]
            for dz in range(1, nz):
                arrive(from_z.at[dx, dy, dz - 1], number((dx, dy, dz)))
                total = total + from_z[dx, dy, dz - 1]
            sum_z[dx, dy] = total
            if dy > 0:
                send(sum_z.at[dx, dy], from_y.at[dx, dy - 1], number((dx, dy, 0)), 1, dy)
    for dx in order_x:
        total = sum_z[dx, 0]
        for dy in range(1, ny):
            arrive(from_y.at[dx, dy - 1], number((dx, dy, 0)))
            total = total + from_y[dx, dy - 1]
        sum_y[dx] = total
        if dx > 0:
            send(sum_y.at[dx], from_x.at[dx - 1], number((dx, 0, 0)), 0, dx)
    for dx in range(1, nx):
        arrive(from_x.at[dx - 1], number((dx, 0, 0)))
        total = total + from_x[dx - 1]
    square = total * total
    part = jnp.zeros((8, 128), jnp.float32)
    for i in range(0, square.shape[0], 8):
        for j in range(0, square.shape[1], 128):
            part = part + square[i : i + 8, j : j + 128]
    slot = 0
    for axis in range(3):
        parts[slot] = part
        copies = []
        for step in range(1, sizes[axis]):
            copy = transfer(
                parts.at[slot],
                parts.at[slot + step],
                small_s.at[slot + step],
                small_r.at[slot + step],
                shifted(axis, step),
            )
            copy.start()
            copies.append(copy)
        for step in range(1, sizes[axis]):
            copies[step - 1].wait_recv()
            part = part + parts[slot + step]
        started.extend(copies)
        slot += sizes[axis]
    overall = jnp.sum(part, keepdims=True)
    count_all = nx * ny * nz * total.size
    scaled = total * lax.rsqrt(overall / count_all + NORM_EPS)
    out_first[...] = scaled[:ENC]
    out_head[...] = scaled[ENC:]
    for copy in started:
        copy.wait_send()


def sum_and_scale(grads, sizes):
    nx, ny, nz = sizes
    count = nx * ny * nz
    tile = grads.shape[1:]
    vmem = pl.BlockSpec(memory_space=pltpu.VMEM)
    small = nx + ny + nz
    return pl.pallas_call(
        functools.partial(update_kernel, sizes),
        out_shape=(
            jax.ShapeDtypeStruct((ENC, tile[1]), jnp.float32),
            jax.ShapeDtypeStruct((tile[0] - ENC, tile[1]), jnp.float32),
        ),
        in_specs=[vmem],
        out_specs=(vmem, vmem),
        scratch_shapes=[
            pltpu.VMEM((nx, ny, max(nz - 1, 1)) + tile, jnp.float32),
            pltpu.VMEM((nx, ny) + tile, jnp.float32),
            pltpu.VMEM((nx, max(ny - 1, 1)) + tile, jnp.float32),
            pltpu.VMEM((nx,) + tile, jnp.float32),
            pltpu.VMEM((max(nx - 1, 1),) + tile, jnp.float32),
            pltpu.VMEM((small, 8, 128), jnp.float32),
            pltpu.SemaphoreType.DMA((count,)),
            pltpu.SemaphoreType.DMA((count,)),
            pltpu.SemaphoreType.DMA((small,)),
            pltpu.SemaphoreType.DMA((small,)),
        ],
        compiler_params=pltpu.CompilerParams(
            collective_id=1, has_side_effects=True, vmem_limit_bytes=VMEM_BYTES
        ),
        name="sum_and_scale",
    )(grads.reshape(sizes + tile))


def by_gather(positions, spacing, crossings, target, first_weight, head_weight):
    sizes = tuple(lax.axis_size(name) for name in AXES)
    gathered, rest = gather_weights(
        first_weight[0].T, head_weight[0], positions, spacing, crossings, sizes
    )
    rendered, grads = own_rays(gathered, *rest, target)
    first, head = sum_and_scale(grads, sizes)
    return (rendered, first.T[None], head[None])


def encode(points):
    scales = 2.0 ** jnp.arange(FREQS, dtype=jnp.float32) * PI_VALUE
    angles = scales[:, None, None] * points[None]
    wave_table = jnp.stack([jnp.sin(angles), jnp.cos(angles)], axis=1)
    return wave_table.reshape(6 * FREQS, points.shape[1]).astype(jnp.bfloat16)


def network(first_local, head_local, points):
    encoded = encode(points)
    before = jnp.dot(first_local, encoded, preferred_element_type=jnp.float32)
    hidden = jax.nn.silu(before).astype(jnp.bfloat16)
    output = jnp.dot(head_local, hidden, preferred_element_type=jnp.float32)
    return (encoded, before, hidden, output)


def activate(output):
    return (jax.nn.softplus(output[0]), jax.nn.sigmoid(output[1:]))


def segment_forward(density, colour, step_len):
    optical = density * step_len[:, None]
    inclusive = jnp.cumsum(optical, axis=1)
    leaving = jnp.exp(-inclusive)
    weight = jnp.exp(optical - inclusive) - leaving
    seg_colour = jnp.sum(weight[None] * colour, axis=2)
    return (seg_colour, leaving[:, -1], weight, leaving)


def segment_backward(colour, weight, leaving, step_len, grad_colour, grad_trans):
    shading = jnp.sum(colour * grad_colour[:, :, None], axis=0)
    weighted = weight * shading
    after = jnp.sum(weighted, axis=1, keepdims=True) - jnp.cumsum(weighted, axis=1)
    grad_depth = shading * leaving - after - (grad_trans * leaving[:, -1])[:, None]
    grad_density = grad_depth * step_len[:, None]
    grad_sample = weight[None] * grad_colour[:, :, None]
    return (grad_density, grad_sample)


def ray_level(seg_colour, seg_trans, target):
    seg_total = seg_trans.shape[1]
    through = jnp.cumprod(seg_trans, axis=1)
    prefix = jnp.concatenate([jnp.ones_like(seg_trans[:, :1]), through[:, :-1]], axis=1)
    rendered = jnp.sum(prefix[None] * seg_colour, axis=2)
    residual = rendered - target
    grad_colour = prefix[None] * residual[:, :, None]
    behind_list = [jnp.zeros_like(rendered)]
    for offset in range(seg_total - 1, 0, -1):
        behind_list.append(seg_colour[:, :, offset] + seg_trans[:, offset][None] * behind_list[-1])
    behind = jnp.stack(behind_list[::-1], axis=2)
    grad_trans = prefix * jnp.sum(behind * residual[:, :, None], axis=0)
    return (rendered, grad_colour, grad_trans)


def output_grad(output, grad_density, grad_sample):
    colour = jax.nn.sigmoid(output[1:])
    first_row = grad_density * jax.nn.sigmoid(output[0])
    others = grad_sample * colour * (1.0 - colour)
    return jnp.concatenate([first_row[None], others], axis=0).astype(jnp.bfloat16)


def network_grad(head_local, encoded, before, hidden, upstream):
    grad_head = lax.dot_general(
        upstream, hidden, (((1,), (1,)), ((), ())), preferred_element_type=jnp.float32
    )
    grad_hidden = lax.dot_general(
        head_local, upstream, (((0,), (0,)), ((), ())), preferred_element_type=jnp.float32
    )
    logistic = jax.nn.sigmoid(before)
    grad_before = (grad_hidden * logistic * (1.0 + before * (1.0 - logistic))).astype(jnp.bfloat16)
    grad_first = lax.dot_general(
        grad_before, encoded, (((1,), (1,)), ((), ())), preferred_element_type=jnp.float32
    )
    return (grad_first, grad_head)


def by_exchange(positions, spacing, crossings, target, first_weight, head_weight):
    across = lax.axis_size(("gx", "gy"))
    along_count = lax.axis_size("gz")
    devices = across * along_count
    ray_rows = crossings.shape[0]
    entries = ray_rows * SEGS
    capacity = 2 * entries // devices
    total_slots = devices * capacity
    sample_total = total_slots * SAMPLES
    block_size = math.gcd(sample_total, BLOCK_LIMIT)
    block_count = sample_total // block_size
    block_segs = block_size // SAMPLES
    first_local = first_weight[0]
    head_local = head_weight[0]
    brick_ids = crossings.reshape(entries)
    order_rank = jnp.arange(entries, dtype=jnp.int32)
    earlier = (brick_ids[:, None] == brick_ids[None, :]) & (
        order_rank[None, :] < order_rank[:, None]
    )
    column = brick_ids * capacity + jnp.sum(earlier.astype(jnp.int32), axis=1)
    own_points = positions.reshape(3, entries, SAMPLES)
    own_steps = spacing.reshape(entries)
    send_points = jnp.zeros((3, total_slots, SAMPLES), jnp.float32).at[:, column, :].set(own_points)
    send_steps = jnp.zeros((1, total_slots), jnp.float32).at[0, column].set(own_steps)
    got_points, got_steps = (
        lax.all_to_all(
            lax.all_to_all(
                send_points.reshape(3, across, along_count, capacity * SAMPLES),
                ("gx", "gy"),
                split_axis=1,
                concat_axis=1,
                tiled=True,
            ),
            "gz",
            split_axis=2,
            concat_axis=2,
            tiled=True,
        ),
        lax.all_to_all(
            lax.all_to_all(
                send_steps.reshape(1, across, along_count, capacity),
                ("gx", "gy"),
                split_axis=1,
                concat_axis=1,
                tiled=True,
            ),
            "gz",
            split_axis=2,
            concat_axis=2,
            tiled=True,
        ),
    )
    point_blocks = got_points.reshape(3, block_count, block_size).transpose(1, 0, 2)
    step_blocks = got_steps.reshape(block_count, block_segs)

    def forward_turn(unused, inputs):
        block_points, block_steps = inputs
        encoded, before, hidden, output = network(first_local, head_local, block_points)
        density, colour = activate(output)
        result = jnp.concatenate([density[None], colour], axis=0)
        return (unused, result)

    unused, results = lax.scan(
        forward_turn, jnp.zeros((), jnp.float32), (point_blocks, step_blocks)
    )
    values = results.transpose(1, 0, 2).reshape(4, across, along_count, capacity * SAMPLES)
    returned = lax.all_to_all(
        lax.all_to_all(values, ("gx", "gy"), split_axis=1, concat_axis=1, tiled=True),
        "gz",
        split_axis=2,
        concat_axis=2,
        tiled=True,
    )
    owned = returned.reshape(4, total_slots, SAMPLES)[:, column, :]
    seg_colour, seg_trans, weight, leaving = segment_forward(owned[0], owned[1:], own_steps)
    rendered, grad_colour, grad_trans = ray_level(
        seg_colour.reshape(3, ray_rows, SEGS), seg_trans.reshape(ray_rows, SEGS), target
    )
    grad_density, grad_sample = segment_backward(
        owned[1:],
        weight,
        leaving,
        own_steps,
        grad_colour.reshape(3, entries),
        grad_trans.reshape(entries),
    )
    stacked = jnp.concatenate([grad_density[None], grad_sample], axis=0)
    send_grads = jnp.zeros((4, total_slots, SAMPLES), jnp.float32).at[:, column, :].set(stacked)
    got_grads = lax.all_to_all(
        lax.all_to_all(
            send_grads.reshape(4, across, along_count, capacity * SAMPLES),
            ("gx", "gy"),
            split_axis=1,
            concat_axis=1,
            tiled=True,
        ),
        "gz",
        split_axis=2,
        concat_axis=2,
        tiled=True,
    )
    grad_blocks = got_grads.reshape(4, block_count, block_size).transpose(1, 0, 2)

    def backward_turn(totals, inputs):
        block_points, block_steps, block_upstream = inputs
        encoded, before, hidden, output = network(first_local, head_local, block_points)
        grad_density = block_upstream[0]
        grad_sample = block_upstream[1:]
        upstream = output_grad(output, grad_density, grad_sample)
        grad_first, grad_head = network_grad(head_local, encoded, before, hidden, upstream)
        return ((totals[0] + grad_first, totals[1] + grad_head), None)

    start_totals = (
        jnp.zeros(first_local.shape, jnp.float32),
        jnp.zeros(head_local.shape, jnp.float32),
    )
    totals, unused_out = lax.scan(
        backward_turn, start_totals, (point_blocks, step_blocks, grad_blocks)
    )
    grad_first, grad_head = totals
    square_sum = jnp.sum(grad_first * grad_first) + jnp.sum(grad_head * grad_head)
    overall = lax.psum(square_sum, ("gx", "gy", "gz"))
    count_all = devices * (grad_first.size + grad_head.size)
    scale = lax.rsqrt(overall / count_all + NORM_EPS)
    return (rendered, (grad_first * scale)[None], (grad_head * scale)[None])


def solution(mesh):
    in_specs = (
        P(None, ("gx", "gy", "gz"), None),
        P(("gx", "gy", "gz"), None),
        P(("gx", "gy", "gz"), None),
        P(None, ("gx", "gy", "gz")),
        P(("gx", "gy", "gz"), None, None),
        P(("gx", "gy", "gz"), None, None),
    )
    out_specs = (
        P(None, ("gx", "gy", "gz")),
        P(("gx", "gy", "gz"), None, None),
        P(("gx", "gy", "gz"), None, None),
    )
    body = by_gather if mesh.size <= GATHER_LIMIT else by_exchange
    return jax.shard_map(
        body, mesh=mesh, in_specs=in_specs, out_specs=out_specs, check_vma=False
    )
```

```python
import functools
import math

import jax
import jax.numpy as jnp
from jax import lax
from jax.experimental import pallas as pl
from jax.experimental.pallas import tpu as pltpu
from jax.sharding import PartitionSpec as P

FREQS = 10
SAMPLES = 64
SEGS = 8
AXES = ("gx", "gy", "gz")
ENC = 6 * FREQS
ROWS = ENC + 4
HID = 256
PACK = 4
LANES = PACK * SAMPLES
GATHER_LIMIT = 64
VMEM_BYTES = 58 * 1024 * 1024


PI_VALUE = 3.141592653589793
NORM_EPS = 1e-06
BLOCK_LIMIT = 2048


def in_parts(x):
    parts = []
    for _ in range(3):
        parts.append(x.astype(jnp.bfloat16))
        x = x - parts[-1].astype(jnp.float32)
    return parts


def mask_times(mask, x):
    mask = mask.astype(jnp.bfloat16)
    return sum(
        jnp.dot(mask, part, preferred_element_type=jnp.float32) for part in in_parts(x)[::-1]
    )


def times_mask(x, mask):
    mask = mask.astype(jnp.bfloat16)
    return sum(
        jnp.dot(part, mask, preferred_element_type=jnp.float32) for part in in_parts(x)[::-1]
    )


def iota(shape, dim):
    return lax.broadcasted_iota(jnp.int32, shape, dim)


def logistic(x):
    return 0.5 + 0.5 * jnp.tanh(0.5 * x)


def encode_block(p0, p1, p2):
    shape = (ROWS, LANES)
    row = iota((ROWS, 1), 0)
    freq = row // 6
    axis = row % 3
    scale = jnp.zeros((ROWS, 1), jnp.float32)
    for k in range(FREQS):
        scale = jnp.where(freq == k, 2.0 ** (k - 1), scale)
    is_cos = (row % 6 // 3 == 1) & (row < ENC)
    shift = jnp.where(is_cos, 0.0, 0.25)
    point = jnp.where(
        axis == 0,
        jnp.broadcast_to(p0, shape),
        jnp.where(axis == 1, jnp.broadcast_to(p1, shape), jnp.broadcast_to(p2, shape)),
    )
    turns = point * scale - shift
    arg = 0.25 - jnp.abs(turns - jnp.round(turns))
    square = arg * arg
    circle = 2.0 * PI_VALUE
    total = jnp.full(shape, -(circle**11) / math.factorial(11), jnp.float32)
    for power in (9, 7, 5, 3, 1):
        factor = circle**power / math.factorial(power)
        total = total * square + (factor if power % 4 == 1 else -factor)
    return (total * arg).astype(jnp.bfloat16)


def to_column(row):
    n = row.shape[1]
    return jnp.sum(jnp.where(iota((n, n), 0) == iota((n, n), 1), row, 0.0), axis=1, keepdims=True)


def to_row(column):
    n = column.shape[0]
    return jnp.sum(
        jnp.where(iota((n, n), 0) == iota((n, n), 1), column, 0.0), axis=0, keepdims=True
    )


def number_groups(bricks, crossings, group_row, group_col, place_col, brick_of):
    ids_col = jnp.concatenate(
        [to_column(crossings[s : s + 1, :].astype(jnp.float32)) for s in range(SEGS)], axis=0
    )
    entries = ids_col.shape[0]
    ids_row = to_row(ids_col)
    square = (entries, entries)
    same = ids_col == ids_row
    rank_col = jnp.sum(
        jnp.where(same & (iota(square, 1) < iota(square, 0)), 1.0, 0.0), axis=1, keepdims=True
    )
    rank_row = jnp.sum(
        jnp.where(same & (iota(square, 0) < iota(square, 1)), 1.0, 0.0), axis=0, keepdims=True
    )
    wide = 128
    of_brick = ids_col == iota((entries, wide), 1).astype(jnp.float32)
    counts = jnp.sum(jnp.where(of_brick, 1.0, 0.0), axis=0, keepdims=True)
    needed_row = jnp.floor((counts + (PACK - 1)) * (1.0 / PACK))
    needed_col = to_column(needed_row)
    pair = (wide, wide)
    start_row = jnp.sum(
        jnp.where(iota(pair, 0) < iota(pair, 1), needed_col, 0.0), axis=0, keepdims=True
    )
    start_col = to_column(start_row)
    first_col = jnp.sum(jnp.where(of_brick, start_row, 0.0), axis=1, keepdims=True)
    of_brick_t = ids_row == iota((wide, entries), 0).astype(jnp.float32)
    first_row = jnp.sum(jnp.where(of_brick_t, start_col, 0.0), axis=0, keepdims=True)
    full_col = jnp.floor(rank_col * (1.0 / PACK))
    full_row = jnp.floor(rank_row * (1.0 / PACK))
    group_col[...] = (first_col + full_col).astype(jnp.int32)
    group_row[...] = (first_row + full_row).astype(jnp.int32)
    place_col[...] = (rank_col - PACK * full_col).astype(jnp.int32)
    shape = (wide, brick_of.shape[1])
    number = iota(shape, 1).astype(jnp.float32)
    passed = (start_col + needed_col <= number) & (iota(shape, 0) < bricks)
    found = jnp.sum(jnp.where(passed, 1.0, 0.0), axis=0, keepdims=True)
    total = jnp.sum(needed_row, axis=1, keepdims=True)
    last = iota(brick_of.shape, 1) == brick_of.shape[1] - 1
    brick_of[...] = jnp.where(last, total, jnp.minimum(found, bricks - 1.0)).astype(jnp.int32)


def place_points(groups, positions, spacing, group_row, place_col, points, steps):
    ray_rows = positions.shape[1]
    entries = ray_rows * SEGS
    place = (iota((groups, entries), 0) == group_row[...]).astype(jnp.float32)
    chosen = place_col[...] == iota((entries, LANES), 1) // SAMPLES
    low = iota((ray_rows, 2 * SAMPLES), 1) < SAMPLES
    for c in range(3):
        parts = []
        for pair in range(SEGS // 2):
            both = positions[c, :, 2 * SAMPLES * pair : 2 * SAMPLES * (pair + 1)]
            turned = pltpu.roll(both, SAMPLES, 1)
            for half in (jnp.where(low, both, turned), jnp.where(low, turned, both)):
                parts.append(jnp.concatenate([half] * (LANES // (2 * SAMPLES)), axis=1))
        values = jnp.where(chosen, jnp.concatenate(parts, axis=0), 0.0)
        points[c] = mask_times(place, values)
    lengths = jnp.concatenate(
        [to_column(spacing[s : s + 1, :]) for s in range(SEGS)], axis=0
    )
    steps[...] = mask_times(place, jnp.where(chosen, lengths, 0.0))


def rays_kernel(
    groups,
    bricks,
    ray_rows,
    brick_list,
    weights,
    encoded_in,
    steps_in,
    group_row,
    group_col,
    place_col,
    target,
    rendered_out,
    grads,
    weight_t,
    hidden,
    slope,
    outs,
    ups,
    per_entry,
    encoded,
    arrived,
):
    fetch = pltpu.make_async_copy(encoded_in, encoded, arrived)
    fetch.start()
    entries = ray_rows * SEGS
    together = 8
    turns = (brick_list[0, brick_list.shape[1] - 1] + together - 1) // together
    place = (iota((groups, entries), 0) == group_row[...]).astype(jnp.float32)
    outs[...] = jnp.zeros_like(outs)
    grads[...] = jnp.zeros_like(grads)

    few = math.gcd(bricks, 4)

    @pl.loop(0, bricks // few)
    def _(turn):
        for i in range(few):
            weight_t[few * turn + i] = (0.5 * weights[few * turn + i].T).astype(jnp.bfloat16)

    fetch.wait()

    def forward(g):
        b = brick_list[0, g]
        half = jnp.dot(weight_t[b], encoded[g], preferred_element_type=jnp.float32)
        bent = jnp.tanh(half)
        act = half + half * bent
        slope[g] = ((1.0 + act) + bent * (1.0 - act)).astype(jnp.bfloat16)
        hid = act.astype(jnp.bfloat16)
        hidden[g] = hid
        head = weights[b, ROWS - 8 :, :].astype(jnp.bfloat16)
        out = jnp.dot(head, hid, preferred_element_type=jnp.float32)
        for ch in range(4):
            outs[ch, pl.ds(g, 1), :] = out[4 + ch : 5 + ch, :]

    @pl.loop(0, turns)
    def _(turn):
        for i in range(together):
            forward(together * turn + i)

    same = iota((LANES, LANES), 0) // SAMPLES == iota((LANES, LANES), 1) // SAMPLES
    upto = (same & (iota((LANES, LANES), 0) <= iota((LANES, LANES), 1))).astype(jnp.float32)
    beyond = (same & (iota((LANES, LANES), 0) > iota((LANES, LANES), 1))).astype(jnp.float32)
    steps = steps_in[...]
    raw = outs[0]
    density = jnp.maximum(raw, 0.0) + jnp.log1p(jnp.exp(-jnp.abs(raw)))
    colour = [logistic(outs[1 + c]) for c in range(3)]
    optical = density * steps
    inclusive = times_mask(optical, upto)
    leaving = jnp.exp(-inclusive)
    weight = jnp.exp(optical - inclusive) - leaving
    lane = iota((LANES, 128), 0)
    col = iota((LANES, 128), 1)
    sums = jnp.zeros((groups, 128), jnp.float32)
    for ch in range(4):
        pick = col == 4 * ch + lane // SAMPLES
        if ch == 3:
            pick = pick & (lane % SAMPLES == SAMPLES - 1)
        sums = sums + times_mask(weight * colour[ch] if ch < 3 else leaving, pick.astype(jnp.float32))
    back = (iota((entries, groups), 1) == group_col[...]).astype(jnp.float32)
    found = mask_times(back, sums)
    entry_col = iota((entries, 128), 1)
    here = entry_col % 4 == place_col[...]
    values = [
        jnp.sum(jnp.where(here & (entry_col // 4 == ch), found, 0.0), axis=1, keepdims=True)
        for ch in range(4)
    ]

    def seg(ch, s):
        return values[ch][s * ray_rows : (s + 1) * ray_rows]

    prefix = [jnp.ones((ray_rows, 1), jnp.float32)]
    for s in range(SEGS - 1):
        prefix.append(prefix[s] * seg(3, s))
    residual = []
    for c in range(3):
        shown = sum(prefix[s] * seg(c, s) for s in range(SEGS))
        rendered_out[c : c + 1, :] = to_row(shown)
        residual.append(shown - to_column(target[c : c + 1, :]))
    behind = [jnp.zeros((ray_rows, 1), jnp.float32)] * 3
    for s in range(SEGS - 1, -1, -1):
        grad_trans = prefix[s] * sum(behind[c] * residual[c] for c in range(3))
        rows = pl.ds(s * ray_rows, ray_rows)
        mine = here[s * ray_rows : (s + 1) * ray_rows]
        which = entry_col[s * ray_rows : (s + 1) * ray_rows] // 4
        block = jnp.zeros((ray_rows, 128), jnp.float32)
        for ch in range(4):
            value = prefix[s] * residual[ch] if ch < 3 else grad_trans * seg(3, s)
            block = jnp.where(mine & (which == ch), value, block)
        per_entry[rows, :] = block
        behind = [seg(c, s) + seg(3, s) * behind[c] for c in range(3)]
    spread = mask_times(place, per_entry[...])
    wide = []
    for ch in range(4):
        to_lanes = iota((128, LANES), 0) == 4 * ch + iota((128, LANES), 1) // SAMPLES
        wide.append(times_mask(spread, to_lanes.astype(jnp.float32)))
    shading = sum(colour[c] * wide[c] for c in range(3))
    after = times_mask(weight * shading, beyond)
    ups[0] = (shading * leaving - after - wide[3]) * steps * logistic(raw)
    for c in range(3):
        ups[1 + c] = weight * wide[c] * colour[c] * (1.0 - colour[c])

    row8 = iota((8, LANES), 0)

    def backward(g):
        b = brick_list[0, g]
        up8 = jnp.zeros((8, LANES), jnp.float32)
        for ch in range(4):
            line = jnp.broadcast_to(ups[ch, pl.ds(g, 1), :], (8, LANES))
            up8 = jnp.where(row8 == 4 + ch, line, up8)
        up16 = jnp.concatenate([jnp.zeros((8, LANES), jnp.float32), up8], axis=0)
        up16 = up16.astype(jnp.bfloat16)
        up = jnp.concatenate([jnp.zeros((ROWS - 16, LANES), jnp.bfloat16), up16], axis=0)
        grad_hidden = jnp.dot(weight_t[b], up, preferred_element_type=jnp.float32)
        grad_before = (grad_hidden * slope[g].astype(jnp.float32)).astype(jnp.bfloat16)
        dims = (((1,), (1,)), ((), ()))
        first = lax.dot_general(
            encoded[g], grad_before, dims, preferred_element_type=jnp.float32
        )
        last = lax.dot_general(up16, hidden[g], dims, preferred_element_type=jnp.float32)
        return first[: ROWS - 16], first[ROWS - 16 :] + last

    @pl.loop(0, turns)
    def _(turn):
        terms = [backward(together * turn + i) for i in range(together)]
        for i in range(together):
            b = brick_list[0, together * turn + i]
            grads[b, : ROWS - 16, :] += terms[i][0]
            grads[b, ROWS - 16 :, :] += terms[i][1]


def own_rays(gathered, encoded, steps, group_row, group_col, place_col, brick_of, target):
    bricks = gathered.shape[0]
    ray_rows = target.shape[1]
    entries = ray_rows * SEGS
    groups = encoded.shape[0]
    vmem = pl.BlockSpec(memory_space=pltpu.VMEM)
    samples = groups * LANES
    return pl.pallas_call(
        functools.partial(rays_kernel, groups, bricks, ray_rows),
        out_shape=(
            jax.ShapeDtypeStruct((3, ray_rows), jnp.float32),
            jax.ShapeDtypeStruct((bricks, ROWS, HID), jnp.float32),
        ),
        in_specs=[
            pl.BlockSpec(memory_space=pltpu.SMEM),
            vmem,
            pl.BlockSpec(memory_space=pl.ANY),
        ]
        + [vmem] * 5,
        out_specs=(vmem, vmem),
        scratch_shapes=[
            pltpu.VMEM((bricks, HID, ROWS), jnp.bfloat16),
            pltpu.VMEM((groups, HID, LANES), jnp.bfloat16),
            pltpu.VMEM((groups, HID, LANES), jnp.bfloat16),
            pltpu.VMEM((4, groups, LANES), jnp.float32),
            pltpu.VMEM((4, groups, LANES), jnp.float32),
            pltpu.VMEM((entries, 128), jnp.float32),
            pltpu.VMEM(encoded.shape, encoded.dtype),
            pltpu.SemaphoreType.DMA(()),
        ],
        compiler_params=pltpu.CompilerParams(vmem_limit_bytes=VMEM_BYTES),
        cost_estimate=pl.CostEstimate(
            flops=samples * HID * ROWS * 10,
            transcendentals=samples * HID,
            bytes_accessed=2 * bricks * ROWS * HID * 4,
        ),
        name="own_rays",
    )(brick_of, gathered, encoded, steps, group_row, group_col, place_col, target)


def partners(sizes):
    here = tuple(lax.axis_index(name) for name in AXES)

    def shifted(axis, step):
        place = list(here)
        place[axis] = lax.rem(here[axis] + step, sizes[axis])
        return tuple(place)

    others = [shifted(axis, step) for axis in range(3) for step in range(1, sizes[axis])]
    return here, shifted, others


def greet(others):
    barrier = pltpu.get_barrier_semaphore()
    for other in others:
        pl.semaphore_signal(barrier, inc=1, device_id=other, device_id_type=pl.DeviceIdType.MESH)
    pl.semaphore_wait(barrier, len(others))


def transfer(source, landing, send_sem, recv_sem, device):
    return pltpu.make_async_remote_copy(
        src_ref=source,
        dst_ref=landing,
        send_sem=send_sem,
        recv_sem=recv_sem,
        device_id=device,
        device_id_type=pl.DeviceIdType.MESH,
    )


def gather_kernel(
    sizes,
    groups,
    own_first,
    own_head,
    positions,
    spacing,
    crossings,
    out,
    encoded,
    steps,
    group_row,
    group_col,
    place_col,
    brick_of,
    points,
    sends,
    recvs,
):
    nx, ny, nz = sizes

    def encode_groups(first, end):
        @pl.loop(first, end)
        def _(turn):
            for g in (2 * turn, 2 * turn + 1):
                encoded[g] = encode_block(*[points[c, pl.ds(g, 1), :] for c in range(3)])

    (x, y, z), shifted, others = partners(sizes)
    greet(others)
    out[x, y, z, :ENC, :] = own_first[...].astype(jnp.float32)
    out[x, y, z, ENC:, :] = own_head[...].astype(jnp.float32)
    started = []

    def block(dx, dy, dz):
        return out.at[
            lax.rem(x - dx + nx, nx), lax.rem(y - dy + ny, ny), lax.rem(z - dz + nz, nz)
        ]

    def send(source, axis, step, came):
        where = (came[0] * ny + came[1]) * nz + came[2]
        copy = transfer(source, source, sends.at[where], recvs.at[where], shifted(axis, step))
        copy.start()
        started.append(copy)

    def arrive(came):
        where = (came[0] * ny + came[1]) * nz + came[2]
        landed = block(*came)
        transfer(landed, landed, sends.at[where], recvs.at[where], others[0]).wait_recv()

    for dx in range(1, nx):
        send(block(0, 0, 0), 0, dx, (dx, 0, 0))
    number_groups(nx * ny * nz, crossings, group_row, group_col, place_col, brick_of)
    for dx in range(nx):
        if dx > 0:
            arrive((dx, 0, 0))
        for dy in range(1, ny):
            send(block(dx, 0, 0), 1, dy, (dx, dy, 0))
        for dz in range(1, nz):
            send(block(dx, 0, 0), 2, dz, (dx, 0, dz))
    place_points(groups, positions, spacing, group_row, place_col, points, steps)
    turns = groups // 2
    for dx in range(nx):
        encode_groups(turns * dx // nx, turns * (dx + 1) // nx)
        for dy in range(1, ny):
            arrive((dx, dy, 0))
            for dz in range(1, nz):
                send(block(dx, dy, 0), 2, dz, (dx, dy, dz))
    for dx in range(nx):
        for dy in range(ny):
            for dz in range(1, nz):
                arrive((dx, dy, dz))
    for copy in started:
        copy.wait_send()


def gather_weights(first, head, positions, spacing, crossings, sizes):
    count = sizes[0] * sizes[1] * sizes[2]
    ray_rows = crossings.shape[0]
    entries = ray_rows * SEGS
    groups = -(-((entries + (PACK - 1) * count) // PACK) // 8) * 8
    listed = -(-(groups + 1) // 128) * 128
    vmem = pl.BlockSpec(memory_space=pltpu.VMEM)
    gathered, *rest = pl.pallas_call(
        functools.partial(gather_kernel, sizes, groups),
        out_shape=(
            jax.ShapeDtypeStruct(sizes + (ROWS, HID), jnp.float32),
            jax.ShapeDtypeStruct((groups, ROWS, LANES), jnp.bfloat16),
            jax.ShapeDtypeStruct((groups, LANES), jnp.float32),
            jax.ShapeDtypeStruct((1, entries), jnp.int32),
            jax.ShapeDtypeStruct((entries, 1), jnp.int32),
            jax.ShapeDtypeStruct((entries, 1), jnp.int32),
            jax.ShapeDtypeStruct((1, listed), jnp.int32),
        ),
        in_specs=[vmem] * 5,
        out_specs=[vmem] * 7,
        scratch_shapes=[
            pltpu.VMEM((3, groups, LANES), jnp.float32),
            pltpu.SemaphoreType.DMA((count,)),
            pltpu.SemaphoreType.DMA((count,)),
        ],
        compiler_params=pltpu.CompilerParams(
            collective_id=0, has_side_effects=True, vmem_limit_bytes=VMEM_BYTES
        ),
        name="gather_weights",
    )(first, head, positions, spacing.T, crossings.T)
    return gathered.reshape((count, ROWS, HID)), rest


def update_kernel(
    sizes, grads, out_first, out_head, from_z, sum_z, from_y, sum_y, from_x, parts, sends, recvs, small_s, small_r
):
    nx, ny, nz = sizes
    (x, y, z), shifted, others = partners(sizes)
    greet(others)
    started = []

    def place(step, axis):
        return lax.rem((x, y, z)[axis] + step, sizes[axis])

    def number(step):
        return (step[0] * ny + step[1]) * nz + step[2]

    def send(source, landing, where, axis, step):
        copy = transfer(source, landing, sends.at[where], recvs.at[where], shifted(axis, step))
        copy.start()
        started.append(copy)

    def arrive(landing, where):
        transfer(landing, landing, sends.at[where], recvs.at[where], others[0]).wait_recv()

    order_x = list(range(1, nx)) + [0]
    order_y = list(range(1, ny)) + [0]
    for dx in order_x:
        for dy in order_y:
            for dz in range(1, nz):
                send(
                    grads.at[place(dx, 0), place(dy, 1), place(dz, 2)],
                    from_z.at[dx, dy, dz - 1],
                    number((dx, dy, dz)),
                    2,
                    dz,
                )
    for dx in order_x:
        for dy in order_y:
            total = grads[place(dx, 0), place(dy, 1), z]
            for dz in range(1, nz):
                arrive(from_z.at[dx, dy, dz - 1], number((dx, dy, dz)))
                total = total + from_z[dx, dy, dz - 1]
            sum_z[dx, dy] = total
            if dy > 0:
                send(sum_z.at[dx, dy], from_y.at[dx, dy - 1], number((dx, dy, 0)), 1, dy)
    for dx in order_x:
        total = sum_z[dx, 0]
        for dy in range(1, ny):
            arrive(from_y.at[dx, dy - 1], number((dx, dy, 0)))
            total = total + from_y[dx, dy - 1]
        sum_y[dx] = total
        if dx > 0:
            send(sum_y.at[dx], from_x.at[dx - 1], number((dx, 0, 0)), 0, dx)
    for dx in range(1, nx):
        arrive(from_x.at[dx - 1], number((dx, 0, 0)))
        total = total + from_x[dx - 1]
    square = total * total
    part = jnp.zeros((8, 128), jnp.float32)
    for i in range(0, square.shape[0], 8):
        for j in range(0, square.shape[1], 128):
            part = part + square[i : i + 8, j : j + 128]
    slot = 0
    for axis in range(3):
        parts[slot] = part
        copies = []
        for step in range(1, sizes[axis]):
            copy = transfer(
                parts.at[slot],
                parts.at[slot + step],
                small_s.at[slot + step],
                small_r.at[slot + step],
                shifted(axis, step),
            )
            copy.start()
            copies.append(copy)
        for step in range(1, sizes[axis]):
            copies[step - 1].wait_recv()
            part = part + parts[slot + step]
        started.extend(copies)
        slot += sizes[axis]
    overall = jnp.sum(part, keepdims=True)
    count_all = nx * ny * nz * total.size
    scaled = total * lax.rsqrt(overall / count_all + NORM_EPS)
    out_first[...] = scaled[:ENC]
    out_head[...] = scaled[ENC:]
    for copy in started:
        copy.wait_send()


def sum_and_scale(grads, sizes):
    nx, ny, nz = sizes
    count = nx * ny * nz
    tile = grads.shape[1:]
    vmem = pl.BlockSpec(memory_space=pltpu.VMEM)
    small = nx + ny + nz
    return pl.pallas_call(
        functools.partial(update_kernel, sizes),
        out_shape=(
            jax.ShapeDtypeStruct((ENC, tile[1]), jnp.float32),
            jax.ShapeDtypeStruct((tile[0] - ENC, tile[1]), jnp.float32),
        ),
        in_specs=[vmem],
        out_specs=(vmem, vmem),
        scratch_shapes=[
            pltpu.VMEM((nx, ny, max(nz - 1, 1)) + tile, jnp.float32),
            pltpu.VMEM((nx, ny) + tile, jnp.float32),
            pltpu.VMEM((nx, max(ny - 1, 1)) + tile, jnp.float32),
            pltpu.VMEM((nx,) + tile, jnp.float32),
            pltpu.VMEM((max(nx - 1, 1),) + tile, jnp.float32),
            pltpu.VMEM((small, 8, 128), jnp.float32),
            pltpu.SemaphoreType.DMA((count,)),
            pltpu.SemaphoreType.DMA((count,)),
            pltpu.SemaphoreType.DMA((small,)),
            pltpu.SemaphoreType.DMA((small,)),
        ],
        compiler_params=pltpu.CompilerParams(
            collective_id=1, has_side_effects=True, vmem_limit_bytes=VMEM_BYTES
        ),
        name="sum_and_scale",
    )(grads.reshape(sizes + tile))


def by_gather(positions, spacing, crossings, target, first_weight, head_weight):
    sizes = tuple(lax.axis_size(name) for name in AXES)
    gathered, rest = gather_weights(
        first_weight[0].T, head_weight[0], positions, spacing, crossings, sizes
    )
    rendered, grads = own_rays(gathered, *rest, target)
    first, head = sum_and_scale(grads, sizes)
    return (rendered, first.T[None], head[None])


def encode(points):
    scales = 2.0 ** jnp.arange(FREQS, dtype=jnp.float32) * PI_VALUE
    angles = scales[:, None, None] * points[None]
    wave_table = jnp.stack([jnp.sin(angles), jnp.cos(angles)], axis=1)
    return wave_table.reshape(6 * FREQS, points.shape[1]).astype(jnp.bfloat16)


def network(first_local, head_local, points):
    encoded = encode(points)
    before = jnp.dot(first_local, encoded, preferred_element_type=jnp.float32)
    hidden = jax.nn.silu(before).astype(jnp.bfloat16)
    output = jnp.dot(head_local, hidden, preferred_element_type=jnp.float32)
    return (encoded, before, hidden, output)


def activate(output):
    return (jax.nn.softplus(output[0]), jax.nn.sigmoid(output[1:]))


def segment_forward(density, colour, step_len):
    optical = density * step_len[:, None]
    inclusive = jnp.cumsum(optical, axis=1)
    leaving = jnp.exp(-inclusive)
    weight = jnp.exp(optical - inclusive) - leaving
    seg_colour = jnp.sum(weight[None] * colour, axis=2)
    return (seg_colour, leaving[:, -1], weight, leaving)


def segment_backward(colour, weight, leaving, step_len, grad_colour, grad_trans):
    shading = jnp.sum(colour * grad_colour[:, :, None], axis=0)
    weighted = weight * shading
    after = jnp.sum(weighted, axis=1, keepdims=True) - jnp.cumsum(weighted, axis=1)
    grad_depth = shading * leaving - after - (grad_trans * leaving[:, -1])[:, None]
    grad_density = grad_depth * step_len[:, None]
    grad_sample = weight[None] * grad_colour[:, :, None]
    return (grad_density, grad_sample)


def ray_level(seg_colour, seg_trans, target):
    seg_total = seg_trans.shape[1]
    through = jnp.cumprod(seg_trans, axis=1)
    prefix = jnp.concatenate([jnp.ones_like(seg_trans[:, :1]), through[:, :-1]], axis=1)
    rendered = jnp.sum(prefix[None] * seg_colour, axis=2)
    residual = rendered - target
    grad_colour = prefix[None] * residual[:, :, None]
    behind_list = [jnp.zeros_like(rendered)]
    for offset in range(seg_total - 1, 0, -1):
        behind_list.append(seg_colour[:, :, offset] + seg_trans[:, offset][None] * behind_list[-1])
    behind = jnp.stack(behind_list[::-1], axis=2)
    grad_trans = prefix * jnp.sum(behind * residual[:, :, None], axis=0)
    return (rendered, grad_colour, grad_trans)


def output_grad(output, grad_density, grad_sample):
    colour = jax.nn.sigmoid(output[1:])
    first_row = grad_density * jax.nn.sigmoid(output[0])
    others = grad_sample * colour * (1.0 - colour)
    return jnp.concatenate([first_row[None], others], axis=0).astype(jnp.bfloat16)


def network_grad(head_local, encoded, before, hidden, upstream):
    grad_head = lax.dot_general(
        upstream, hidden, (((1,), (1,)), ((), ())), preferred_element_type=jnp.float32
    )
    grad_hidden = lax.dot_general(
        head_local, upstream, (((0,), (0,)), ((), ())), preferred_element_type=jnp.float32
    )
    logistic = jax.nn.sigmoid(before)
    grad_before = (grad_hidden * logistic * (1.0 + before * (1.0 - logistic))).astype(jnp.bfloat16)
    grad_first = lax.dot_general(
        grad_before, encoded, (((1,), (1,)), ((), ())), preferred_element_type=jnp.float32
    )
    return (grad_first, grad_head)


def by_exchange(positions, spacing, crossings, target, first_weight, head_weight):
    across = lax.axis_size(("gx", "gy"))
    along_count = lax.axis_size("gz")
    devices = across * along_count
    ray_rows = crossings.shape[0]
    entries = ray_rows * SEGS
    capacity = 2 * entries // devices
    total_slots = devices * capacity
    sample_total = total_slots * SAMPLES
    block_size = math.gcd(sample_total, BLOCK_LIMIT)
    block_count = sample_total // block_size
    block_segs = block_size // SAMPLES
    first_local = first_weight[0]
    head_local = head_weight[0]
    brick_ids = crossings.reshape(entries)
    order_rank = jnp.arange(entries, dtype=jnp.int32)
    earlier = (brick_ids[:, None] == brick_ids[None, :]) & (
        order_rank[None, :] < order_rank[:, None]
    )
    column = brick_ids * capacity + jnp.sum(earlier.astype(jnp.int32), axis=1)
    own_points = positions.reshape(3, entries, SAMPLES)
    own_steps = spacing.reshape(entries)
    send_points = jnp.zeros((3, total_slots, SAMPLES), jnp.float32).at[:, column, :].set(own_points)
    send_steps = jnp.zeros((1, total_slots), jnp.float32).at[0, column].set(own_steps)
    got_points, got_steps = (
        lax.all_to_all(
            lax.all_to_all(
                send_points.reshape(3, across, along_count, capacity * SAMPLES),
                ("gx", "gy"),
                split_axis=1,
                concat_axis=1,
                tiled=True,
            ),
            "gz",
            split_axis=2,
            concat_axis=2,
            tiled=True,
        ),
        lax.all_to_all(
            lax.all_to_all(
                send_steps.reshape(1, across, along_count, capacity),
                ("gx", "gy"),
                split_axis=1,
                concat_axis=1,
                tiled=True,
            ),
            "gz",
            split_axis=2,
            concat_axis=2,
            tiled=True,
        ),
    )
    point_blocks = got_points.reshape(3, block_count, block_size).transpose(1, 0, 2)
    step_blocks = got_steps.reshape(block_count, block_segs)

    def forward_turn(unused, inputs):
        block_points, block_steps = inputs
        encoded, before, hidden, output = network(first_local, head_local, block_points)
        density, colour = activate(output)
        result = jnp.concatenate([density[None], colour], axis=0)
        return (unused, result)

    unused, results = lax.scan(
        forward_turn, jnp.zeros((), jnp.float32), (point_blocks, step_blocks)
    )
    values = results.transpose(1, 0, 2).reshape(4, across, along_count, capacity * SAMPLES)
    returned = lax.all_to_all(
        lax.all_to_all(values, ("gx", "gy"), split_axis=1, concat_axis=1, tiled=True),
        "gz",
        split_axis=2,
        concat_axis=2,
        tiled=True,
    )
    owned = returned.reshape(4, total_slots, SAMPLES)[:, column, :]
    seg_colour, seg_trans, weight, leaving = segment_forward(owned[0], owned[1:], own_steps)
    rendered, grad_colour, grad_trans = ray_level(
        seg_colour.reshape(3, ray_rows, SEGS), seg_trans.reshape(ray_rows, SEGS), target
    )
    grad_density, grad_sample = segment_backward(
        owned[1:],
        weight,
        leaving,
        own_steps,
        grad_colour.reshape(3, entries),
        grad_trans.reshape(entries),
    )
    stacked = jnp.concatenate([grad_density[None], grad_sample], axis=0)
    send_grads = jnp.zeros((4, total_slots, SAMPLES), jnp.float32).at[:, column, :].set(stacked)
    got_grads = lax.all_to_all(
        lax.all_to_all(
            send_grads.reshape(4, across, along_count, capacity * SAMPLES),
            ("gx", "gy"),
            split_axis=1,
            concat_axis=1,
            tiled=True,
        ),
        "gz",
        split_axis=2,
        concat_axis=2,
        tiled=True,
    )
    grad_blocks = got_grads.reshape(4, block_count, block_size).transpose(1, 0, 2)

    def backward_turn(totals, inputs):
        block_points, block_steps, block_upstream = inputs
        encoded, before, hidden, output = network(first_local, head_local, block_points)
        grad_density = block_upstream[0]
        grad_sample = block_upstream[1:]
        upstream = output_grad(output, grad_density, grad_sample)
        grad_first, grad_head = network_grad(head_local, encoded, before, hidden, upstream)
        return ((totals[0] + grad_first, totals[1] + grad_head), None)

    start_totals = (
        jnp.zeros(first_local.shape, jnp.float32),
        jnp.zeros(head_local.shape, jnp.float32),
    )
    totals, unused_out = lax.scan(
        backward_turn, start_totals, (point_blocks, step_blocks, grad_blocks)
    )
    grad_first, grad_head = totals
    square_sum = jnp.sum(grad_first * grad_first) + jnp.sum(grad_head * grad_head)
    overall = lax.psum(square_sum, ("gx", "gy", "gz"))
    count_all = devices * (grad_first.size + grad_head.size)
    scale = lax.rsqrt(overall / count_all + NORM_EPS)
    return (rendered, (grad_first * scale)[None], (grad_head * scale)[None])


def solution(mesh):
    in_specs = (
        P(None, ("gx", "gy", "gz"), None),
        P(("gx", "gy", "gz"), None),
        P(("gx", "gy", "gz"), None),
        P(None, ("gx", "gy", "gz")),
        P(("gx", "gy", "gz"), None, None),
        P(("gx", "gy", "gz"), None, None),
    )
    out_specs = (
        P(None, ("gx", "gy", "gz")),
        P(("gx", "gy", "gz"), None, None),
        P(("gx", "gy", "gz"), None, None),
    )
    body = by_gather if mesh.size <= GATHER_LIMIT else by_exchange
    return jax.shard_map(
        body, mesh=mesh, in_specs=in_specs, out_specs=out_specs, check_vma=False
    )
```

```python
import functools
import math

import jax
import jax.numpy as jnp
from jax import lax
from jax.experimental import pallas as pl
from jax.experimental.pallas import tpu as pltpu
from jax.sharding import PartitionSpec as P

FREQS = 10
SAMPLES = 64
SEGS = 8
AXES = ("gx", "gy", "gz")
ENC = 6 * FREQS
ROWS = ENC + 4
HID = 256
PACK = 4
LANES = PACK * SAMPLES
GATHER_LIMIT = 64
VMEM_BYTES = 58 * 1024 * 1024


PI_VALUE = 3.141592653589793
NORM_EPS = 1e-06
BLOCK_LIMIT = 2048


def in_parts(x):
    parts = []
    for _ in range(3):
        parts.append(x.astype(jnp.bfloat16))
        x = x - parts[-1].astype(jnp.float32)
    return parts


def mask_times(mask, x):
    mask = mask.astype(jnp.bfloat16)
    return sum(
        jnp.dot(mask, part, preferred_element_type=jnp.float32) for part in in_parts(x)[::-1]
    )


def times_mask(x, mask):
    mask = mask.astype(jnp.bfloat16)
    return sum(
        jnp.dot(part, mask, preferred_element_type=jnp.float32) for part in in_parts(x)[::-1]
    )


def iota(shape, dim):
    return lax.broadcasted_iota(jnp.int32, shape, dim)


def logistic(x):
    return 0.5 + 0.5 * jnp.tanh(0.5 * x)


def encode_block(p0, p1, p2):
    shape = (ROWS, LANES)
    row = iota((ROWS, 1), 0)
    freq = row // 6
    axis = row % 3
    scale = jnp.zeros((ROWS, 1), jnp.float32)
    for k in range(FREQS):
        scale = jnp.where(freq == k, 2.0 ** (k - 1), scale)
    is_cos = (row % 6 // 3 == 1) & (row < ENC)
    shift = jnp.where(is_cos, 0.0, 0.25)
    point = jnp.where(
        axis == 0,
        jnp.broadcast_to(p0, shape),
        jnp.where(axis == 1, jnp.broadcast_to(p1, shape), jnp.broadcast_to(p2, shape)),
    )
    turns = point * scale - shift
    arg = 0.25 - jnp.abs(turns - jnp.round(turns))
    square = arg * arg
    circle = 2.0 * PI_VALUE
    total = jnp.full(shape, -(circle**11) / math.factorial(11), jnp.float32)
    for power in (9, 7, 5, 3, 1):
        factor = circle**power / math.factorial(power)
        total = total * square + (factor if power % 4 == 1 else -factor)
    return (total * arg).astype(jnp.bfloat16)


def to_column(row):
    n = row.shape[1]
    return jnp.sum(jnp.where(iota((n, n), 0) == iota((n, n), 1), row, 0.0), axis=1, keepdims=True)


def to_row(column):
    n = column.shape[0]
    return jnp.sum(
        jnp.where(iota((n, n), 0) == iota((n, n), 1), column, 0.0), axis=0, keepdims=True
    )


def number_groups(bricks, crossings, group_row, group_col, place_col, brick_of):
    ids_col = jnp.concatenate(
        [to_column(crossings[s : s + 1, :].astype(jnp.float32)) for s in range(SEGS)], axis=0
    )
    entries = ids_col.shape[0]
    ids_row = to_row(ids_col)
    square = (entries, entries)
    same = ids_col == ids_row
    rank_col = jnp.sum(
        jnp.where(same & (iota(square, 1) < iota(square, 0)), 1.0, 0.0), axis=1, keepdims=True
    )
    rank_row = jnp.sum(
        jnp.where(same & (iota(square, 0) < iota(square, 1)), 1.0, 0.0), axis=0, keepdims=True
    )
    wide = 128
    of_brick = ids_col == iota((entries, wide), 1).astype(jnp.float32)
    counts = jnp.sum(jnp.where(of_brick, 1.0, 0.0), axis=0, keepdims=True)
    needed_row = jnp.floor((counts + (PACK - 1)) * (1.0 / PACK))
    needed_col = to_column(needed_row)
    pair = (wide, wide)
    start_row = jnp.sum(
        jnp.where(iota(pair, 0) < iota(pair, 1), needed_col, 0.0), axis=0, keepdims=True
    )
    start_col = to_column(start_row)
    first_col = jnp.sum(jnp.where(of_brick, start_row, 0.0), axis=1, keepdims=True)
    of_brick_t = ids_row == iota((wide, entries), 0).astype(jnp.float32)
    first_row = jnp.sum(jnp.where(of_brick_t, start_col, 0.0), axis=0, keepdims=True)
    full_col = jnp.floor(rank_col * (1.0 / PACK))
    full_row = jnp.floor(rank_row * (1.0 / PACK))
    group_col[...] = (first_col + full_col).astype(jnp.int32)
    group_row[...] = (first_row + full_row).astype(jnp.int32)
    place_col[...] = (rank_col - PACK * full_col).astype(jnp.int32)
    shape = (wide, brick_of.shape[1])
    number = iota(shape, 1).astype(jnp.float32)
    passed = (start_col + needed_col <= number) & (iota(shape, 0) < bricks)
    found = jnp.sum(jnp.where(passed, 1.0, 0.0), axis=0, keepdims=True)
    total = jnp.sum(needed_row, axis=1, keepdims=True)
    last = iota(brick_of.shape, 1) == brick_of.shape[1] - 1
    brick_of[...] = jnp.where(last, total, jnp.minimum(found, bricks - 1.0)).astype(jnp.int32)


def place_points(groups, positions, spacing, group_row, place_col, points, steps):
    ray_rows = positions.shape[1]
    entries = ray_rows * SEGS
    place = (iota((groups, entries), 0) == group_row[...]).astype(jnp.float32)
    chosen = place_col[...] == iota((entries, LANES), 1) // SAMPLES
    low = iota((ray_rows, 2 * SAMPLES), 1) < SAMPLES
    for c in range(3):
        parts = []
        for pair in range(SEGS // 2):
            both = positions[c, :, 2 * SAMPLES * pair : 2 * SAMPLES * (pair + 1)]
            turned = pltpu.roll(both, SAMPLES, 1)
            for half in (jnp.where(low, both, turned), jnp.where(low, turned, both)):
                parts.append(jnp.concatenate([half] * (LANES // (2 * SAMPLES)), axis=1))
        values = jnp.where(chosen, jnp.concatenate(parts, axis=0), 0.0)
        points[c] = mask_times(place, values)
    lengths = jnp.concatenate(
        [to_column(spacing[s : s + 1, :]) for s in range(SEGS)], axis=0
    )
    steps[...] = mask_times(place, jnp.where(chosen, lengths, 0.0))


def rays_kernel(
    groups,
    bricks,
    ray_rows,
    brick_list,
    weights,
    encoded_in,
    steps_in,
    group_row,
    group_col,
    place_col,
    target,
    rendered_out,
    grads,
    weight_t,
    hidden,
    slope,
    outs,
    ups,
    per_entry,
    encoded,
    arrived,
):
    fetch = pltpu.make_async_copy(encoded_in, encoded, arrived)
    fetch.start()
    entries = ray_rows * SEGS
    together = 4
    turns = (brick_list[0, brick_list.shape[1] - 1] + together - 1) // together
    place = (iota((groups, entries), 0) == group_row[...]).astype(jnp.float32)
    outs[...] = jnp.zeros_like(outs)
    grads[...] = jnp.zeros_like(grads)

    few = math.gcd(bricks, 4)

    @pl.loop(0, bricks // few)
    def _(turn):
        for i in range(few):
            weight_t[few * turn + i] = (0.5 * weights[few * turn + i].T).astype(jnp.bfloat16)

    fetch.wait()

    def forward(g):
        b = brick_list[0, g]
        half = jnp.dot(weight_t[b], encoded[g], preferred_element_type=jnp.float32)
        bent = jnp.tanh(half)
        act = half + half * bent
        slope[g] = ((1.0 + act) + bent * (1.0 - act)).astype(jnp.bfloat16)
        hid = act.astype(jnp.bfloat16)
        hidden[g] = hid
        head = weights[b, ROWS - 8 :, :].astype(jnp.bfloat16)
        out = jnp.dot(head, hid, preferred_element_type=jnp.float32)
        for ch in range(4):
            outs[ch, pl.ds(g, 1), :] = out[4 + ch : 5 + ch, :]

    @pl.loop(0, turns)
    def _(turn):
        for i in range(together):
            forward(together * turn + i)

    same = iota((LANES, LANES), 0) // SAMPLES == iota((LANES, LANES), 1) // SAMPLES
    upto = (same & (iota((LANES, LANES), 0) <= iota((LANES, LANES), 1))).astype(jnp.float32)
    beyond = (same & (iota((LANES, LANES), 0) > iota((LANES, LANES), 1))).astype(jnp.float32)
    steps = steps_in[...]
    raw = outs[0]
    density = jnp.maximum(raw, 0.0) + jnp.log1p(jnp.exp(-jnp.abs(raw)))
    colour = [logistic(outs[1 + c]) for c in range(3)]
    optical = density * steps
    inclusive = times_mask(optical, upto)
    leaving = jnp.exp(-inclusive)
    weight = jnp.exp(optical - inclusive) - leaving
    lane = iota((LANES, 128), 0)
    col = iota((LANES, 128), 1)
    sums = jnp.zeros((groups, 128), jnp.float32)
    for ch in range(4):
        pick = col == 4 * ch + lane // SAMPLES
        if ch == 3:
            pick = pick & (lane % SAMPLES == SAMPLES - 1)
        sums = sums + times_mask(weight * colour[ch] if ch < 3 else leaving, pick.astype(jnp.float32))
    back = (iota((entries, groups), 1) == group_col[...]).astype(jnp.float32)
    found = mask_times(back, sums)
    entry_col = iota((entries, 128), 1)
    here = entry_col % 4 == place_col[...]
    values = [
        jnp.sum(jnp.where(here & (entry_col // 4 == ch), found, 0.0), axis=1, keepdims=True)
        for ch in range(4)
    ]

    def seg(ch, s):
        return values[ch][s * ray_rows : (s + 1) * ray_rows]

    prefix = [jnp.ones((ray_rows, 1), jnp.float32)]
    for s in range(SEGS - 1):
        prefix.append(prefix[s] * seg(3, s))
    residual = []
    for c in range(3):
        shown = sum(prefix[s] * seg(c, s) for s in range(SEGS))
        rendered_out[c : c + 1, :] = to_row(shown)
        residual.append(shown - to_column(target[c : c + 1, :]))
    behind = [jnp.zeros((ray_rows, 1), jnp.float32)] * 3
    for s in range(SEGS - 1, -1, -1):
        grad_trans = prefix[s] * sum(behind[c] * residual[c] for c in range(3))
        rows = pl.ds(s * ray_rows, ray_rows)
        mine = here[s * ray_rows : (s + 1) * ray_rows]
        which = entry_col[s * ray_rows : (s + 1) * ray_rows] // 4
        block = jnp.zeros((ray_rows, 128), jnp.float32)
        for ch in range(4):
            value = prefix[s] * residual[ch] if ch < 3 else grad_trans * seg(3, s)
            block = jnp.where(mine & (which == ch), value, block)
        per_entry[rows, :] = block
        behind = [seg(c, s) + seg(3, s) * behind[c] for c in range(3)]
    spread = mask_times(place, per_entry[...])
    wide = []
    for ch in range(4):
        to_lanes = iota((128, LANES), 0) == 4 * ch + iota((128, LANES), 1) // SAMPLES
        wide.append(times_mask(spread, to_lanes.astype(jnp.float32)))
    shading = sum(colour[c] * wide[c] for c in range(3))
    after = times_mask(weight * shading, beyond)
    ups[0] = (shading * leaving - after - wide[3]) * steps * logistic(raw)
    for c in range(3):
        ups[1 + c] = weight * wide[c] * colour[c] * (1.0 - colour[c])

    row8 = iota((8, LANES), 0)

    def backward(g):
        b = brick_list[0, g]
        up8 = jnp.zeros((8, LANES), jnp.float32)
        for ch in range(4):
            line = jnp.broadcast_to(ups[ch, pl.ds(g, 1), :], (8, LANES))
            up8 = jnp.where(row8 == 4 + ch, line, up8)
        up16 = jnp.concatenate([jnp.zeros((8, LANES), jnp.float32), up8], axis=0)
        up16 = up16.astype(jnp.bfloat16)
        up = jnp.concatenate([jnp.zeros((ROWS - 16, LANES), jnp.bfloat16), up16], axis=0)
        grad_hidden = jnp.dot(weight_t[b], up, preferred_element_type=jnp.float32)
        grad_before = (grad_hidden * slope[g].astype(jnp.float32)).astype(jnp.bfloat16)
        dims = (((1,), (1,)), ((), ()))
        first = lax.dot_general(
            encoded[g], grad_before, dims, preferred_element_type=jnp.float32
        )
        last = lax.dot_general(up16, hidden[g], dims, preferred_element_type=jnp.float32)
        grads[b, : ROWS - 16, :] += first[: ROWS - 16]
        grads[b, ROWS - 16 :, :] += first[ROWS - 16 :] + last

    @pl.loop(0, turns)
    def _(turn):
        for i in range(together):
            backward(together * turn + i)


def own_rays(gathered, encoded, steps, group_row, group_col, place_col, brick_of, target):
    bricks = gathered.shape[0]
    ray_rows = target.shape[1]
    entries = ray_rows * SEGS
    groups = encoded.shape[0]
    vmem = pl.BlockSpec(memory_space=pltpu.VMEM)
    samples = groups * LANES
    return pl.pallas_call(
        functools.partial(rays_kernel, groups, bricks, ray_rows),
        out_shape=(
            jax.ShapeDtypeStruct((3, ray_rows), jnp.float32),
            jax.ShapeDtypeStruct((bricks, ROWS, HID), jnp.float32),
        ),
        in_specs=[
            pl.BlockSpec(memory_space=pltpu.SMEM),
            vmem,
            pl.BlockSpec(memory_space=pl.ANY),
        ]
        + [vmem] * 5,
        out_specs=(vmem, vmem),
        scratch_shapes=[
            pltpu.VMEM((bricks, HID, ROWS), jnp.bfloat16),
            pltpu.VMEM((groups, HID, LANES), jnp.bfloat16),
            pltpu.VMEM((groups, HID, LANES), jnp.bfloat16),
            pltpu.VMEM((4, groups, LANES), jnp.float32),
            pltpu.VMEM((4, groups, LANES), jnp.float32),
            pltpu.VMEM((entries, 128), jnp.float32),
            pltpu.VMEM(encoded.shape, encoded.dtype),
            pltpu.SemaphoreType.DMA(()),
        ],
        compiler_params=pltpu.CompilerParams(vmem_limit_bytes=VMEM_BYTES),
        cost_estimate=pl.CostEstimate(
            flops=samples * HID * ROWS * 10,
            transcendentals=samples * HID,
            bytes_accessed=2 * bricks * ROWS * HID * 4,
        ),
        name="own_rays",
    )(brick_of, gathered, encoded, steps, group_row, group_col, place_col, target)


def partners(sizes):
    here = tuple(lax.axis_index(name) for name in AXES)

    def shifted(axis, step):
        place = list(here)
        place[axis] = lax.rem(here[axis] + step, sizes[axis])
        return tuple(place)

    others = [shifted(axis, step) for axis in range(3) for step in range(1, sizes[axis])]
    return here, shifted, others


def greet(others):
    barrier = pltpu.get_barrier_semaphore()
    for other in others:
        pl.semaphore_signal(barrier, inc=1, device_id=other, device_id_type=pl.DeviceIdType.MESH)
    pl.semaphore_wait(barrier, len(others))


def transfer(source, landing, send_sem, recv_sem, device):
    return pltpu.make_async_remote_copy(
        src_ref=source,
        dst_ref=landing,
        send_sem=send_sem,
        recv_sem=recv_sem,
        device_id=device,
        device_id_type=pl.DeviceIdType.MESH,
    )


def gather_kernel(
    sizes,
    groups,
    own_first,
    own_head,
    positions,
    spacing,
    crossings,
    out,
    encoded,
    steps,
    group_row,
    group_col,
    place_col,
    brick_of,
    points,
    sends,
    recvs,
):
    nx, ny, nz = sizes

    def encode_groups(first, end):
        @pl.loop(first, end)
        def _(turn):
            for g in (2 * turn, 2 * turn + 1):
                encoded[g] = encode_block(*[points[c, pl.ds(g, 1), :] for c in range(3)])

    (x, y, z), shifted, others = partners(sizes)
    greet(others)
    out[x, y, z, :ENC, :] = own_first[...].astype(jnp.float32)
    out[x, y, z, ENC:, :] = own_head[...].astype(jnp.float32)
    started = []

    def block(dx, dy, dz):
        return out.at[
            lax.rem(x - dx + nx, nx), lax.rem(y - dy + ny, ny), lax.rem(z - dz + nz, nz)
        ]

    def send(source, axis, step, came):
        where = (came[0] * ny + came[1]) * nz + came[2]
        copy = transfer(source, source, sends.at[where], recvs.at[where], shifted(axis, step))
        copy.start()
        started.append(copy)

    def arrive(came):
        where = (came[0] * ny + came[1]) * nz + came[2]
        landed = block(*came)
        transfer(landed, landed, sends.at[where], recvs.at[where], others[0]).wait_recv()

    for dx in range(1, nx):
        send(block(0, 0, 0), 0, dx, (dx, 0, 0))
    number_groups(nx * ny * nz, crossings, group_row, group_col, place_col, brick_of)
    for dx in range(nx):
        if dx > 0:
            arrive((dx, 0, 0))
        for dy in range(1, ny):
            send(block(dx, 0, 0), 1, dy, (dx, dy, 0))
        for dz in range(1, nz):
            send(block(dx, 0, 0), 2, dz, (dx, 0, dz))
    place_points(groups, positions, spacing, group_row, place_col, points, steps)
    turns = groups // 2
    for dx in range(nx):
        encode_groups(turns * dx // nx, turns * (dx + 1) // nx)
        for dy in range(1, ny):
            arrive((dx, dy, 0))
            for dz in range(1, nz):
                send(block(dx, dy, 0), 2, dz, (dx, dy, dz))
    for dx in range(nx):
        for dy in range(ny):
            for dz in range(1, nz):
                arrive((dx, dy, dz))
    for copy in started:
        copy.wait_send()


def gather_weights(first, head, positions, spacing, crossings, sizes):
    count = sizes[0] * sizes[1] * sizes[2]
    ray_rows = crossings.shape[0]
    entries = ray_rows * SEGS
    groups = -(-((entries + (PACK - 1) * count) // PACK) // 8) * 8
    listed = -(-(groups + 1) // 128) * 128
    vmem = pl.BlockSpec(memory_space=pltpu.VMEM)
    gathered, *rest = pl.pallas_call(
        functools.partial(gather_kernel, sizes, groups),
        out_shape=(
            jax.ShapeDtypeStruct(sizes + (ROWS, HID), jnp.float32),
            jax.ShapeDtypeStruct((groups, ROWS, LANES), jnp.bfloat16),
            jax.ShapeDtypeStruct((groups, LANES), jnp.float32),
            jax.ShapeDtypeStruct((1, entries), jnp.int32),
            jax.ShapeDtypeStruct((entries, 1), jnp.int32),
            jax.ShapeDtypeStruct((entries, 1), jnp.int32),
            jax.ShapeDtypeStruct((1, listed), jnp.int32),
        ),
        in_specs=[vmem] * 5,
        out_specs=[vmem] * 7,
        scratch_shapes=[
            pltpu.VMEM((3, groups, LANES), jnp.float32),
            pltpu.SemaphoreType.DMA((count,)),
            pltpu.SemaphoreType.DMA((count,)),
        ],
        compiler_params=pltpu.CompilerParams(
            collective_id=0, has_side_effects=True, vmem_limit_bytes=VMEM_BYTES
        ),
        name="gather_weights",
    )(first, head, positions, spacing.T, crossings.T)
    return gathered.reshape((count, ROWS, HID)), rest


def update_kernel(
    sizes, grads, out_first, out_head, from_z, sum_z, from_y, sum_y, from_x, parts, sends, recvs, small_s, small_r
):
    nx, ny, nz = sizes
    (x, y, z), shifted, others = partners(sizes)
    greet(others)
    started = []

    def place(step, axis):
        return lax.rem((x, y, z)[axis] + step, sizes[axis])

    def number(step):
        return (step[0] * ny + step[1]) * nz + step[2]

    def send(source, landing, where, axis, step):
        copy = transfer(source, landing, sends.at[where], recvs.at[where], shifted(axis, step))
        copy.start()
        started.append(copy)

    def arrive(landing, where):
        transfer(landing, landing, sends.at[where], recvs.at[where], others[0]).wait_recv()

    order_x = list(range(1, nx)) + [0]
    order_y = list(range(1, ny)) + [0]
    for dx in order_x:
        for dy in order_y:
            for dz in range(1, nz):
                send(
                    grads.at[place(dx, 0), place(dy, 1), place(dz, 2)],
                    from_z.at[dx, dy, dz - 1],
                    number((dx, dy, dz)),
                    2,
                    dz,
                )
    for dx in order_x:
        for dy in order_y:
            total = grads[place(dx, 0), place(dy, 1), z]
            for dz in range(1, nz):
                arrive(from_z.at[dx, dy, dz - 1], number((dx, dy, dz)))
                total = total + from_z[dx, dy, dz - 1]
            sum_z[dx, dy] = total
            if dy > 0:
                send(sum_z.at[dx, dy], from_y.at[dx, dy - 1], number((dx, dy, 0)), 1, dy)
    for dx in order_x:
        total = sum_z[dx, 0]
        for dy in range(1, ny):
            arrive(from_y.at[dx, dy - 1], number((dx, dy, 0)))
            total = total + from_y[dx, dy - 1]
        sum_y[dx] = total
        if dx > 0:
            send(sum_y.at[dx], from_x.at[dx - 1], number((dx, 0, 0)), 0, dx)
    for dx in range(1, nx):
        arrive(from_x.at[dx - 1], number((dx, 0, 0)))
        total = total + from_x[dx - 1]
    square = total * total
    part = jnp.zeros((8, 128), jnp.float32)
    for i in range(0, square.shape[0], 8):
        for j in range(0, square.shape[1], 128):
            part = part + square[i : i + 8, j : j + 128]
    slot = 0
    for axis in range(3):
        parts[slot] = part
        copies = []
        for step in range(1, sizes[axis]):
            copy = transfer(
                parts.at[slot],
                parts.at[slot + step],
                small_s.at[slot + step],
                small_r.at[slot + step],
                shifted(axis, step),
            )
            copy.start()
            copies.append(copy)
        for step in range(1, sizes[axis]):
            copies[step - 1].wait_recv()
            part = part + parts[slot + step]
        started.extend(copies)
        slot += sizes[axis]
    overall = jnp.sum(part, keepdims=True)
    count_all = nx * ny * nz * total.size
    scaled = total * lax.rsqrt(overall / count_all + NORM_EPS)
    out_first[...] = scaled[:ENC]
    out_head[...] = scaled[ENC:]
    for copy in started:
        copy.wait_send()


def sum_and_scale(grads, sizes):
    nx, ny, nz = sizes
    count = nx * ny * nz
    tile = grads.shape[1:]
    vmem = pl.BlockSpec(memory_space=pltpu.VMEM)
    small = nx + ny + nz
    return pl.pallas_call(
        functools.partial(update_kernel, sizes),
        out_shape=(
            jax.ShapeDtypeStruct((ENC, tile[1]), jnp.float32),
            jax.ShapeDtypeStruct((tile[0] - ENC, tile[1]), jnp.float32),
        ),
        in_specs=[vmem],
        out_specs=(vmem, vmem),
        scratch_shapes=[
            pltpu.VMEM((nx, ny, max(nz - 1, 1)) + tile, jnp.float32),
            pltpu.VMEM((nx, ny) + tile, jnp.float32),
            pltpu.VMEM((nx, max(ny - 1, 1)) + tile, jnp.float32),
            pltpu.VMEM((nx,) + tile, jnp.float32),
            pltpu.VMEM((max(nx - 1, 1),) + tile, jnp.float32),
            pltpu.VMEM((small, 8, 128), jnp.float32),
            pltpu.SemaphoreType.DMA((count,)),
            pltpu.SemaphoreType.DMA((count,)),
            pltpu.SemaphoreType.DMA((small,)),
            pltpu.SemaphoreType.DMA((small,)),
        ],
        compiler_params=pltpu.CompilerParams(
            collective_id=1, has_side_effects=True, vmem_limit_bytes=VMEM_BYTES
        ),
        name="sum_and_scale",
    )(grads.reshape(sizes + tile))


def by_gather(positions, spacing, crossings, target, first_weight, head_weight):
    sizes = tuple(lax.axis_size(name) for name in AXES)
    gathered, rest = gather_weights(
        first_weight[0].T, head_weight[0], positions, spacing, crossings, sizes
    )
    rendered, grads = own_rays(gathered, *rest, target)
    first, head = sum_and_scale(grads, sizes)
    return (rendered, first.T[None], head[None])


def encode(points):
    scales = 2.0 ** jnp.arange(FREQS, dtype=jnp.float32) * PI_VALUE
    angles = scales[:, None, None] * points[None]
    wave_table = jnp.stack([jnp.sin(angles), jnp.cos(angles)], axis=1)
    return wave_table.reshape(6 * FREQS, points.shape[1]).astype(jnp.bfloat16)


def network(first_local, head_local, points):
    encoded = encode(points)
    before = jnp.dot(first_local, encoded, preferred_element_type=jnp.float32)
    hidden = jax.nn.silu(before).astype(jnp.bfloat16)
    output = jnp.dot(head_local, hidden, preferred_element_type=jnp.float32)
    return (encoded, before, hidden, output)


def activate(output):
    return (jax.nn.softplus(output[0]), jax.nn.sigmoid(output[1:]))


def segment_forward(density, colour, step_len):
    optical = density * step_len[:, None]
    inclusive = jnp.cumsum(optical, axis=1)
    leaving = jnp.exp(-inclusive)
    weight = jnp.exp(optical - inclusive) - leaving
    seg_colour = jnp.sum(weight[None] * colour, axis=2)
    return (seg_colour, leaving[:, -1], weight, leaving)


def segment_backward(colour, weight, leaving, step_len, grad_colour, grad_trans):
    shading = jnp.sum(colour * grad_colour[:, :, None], axis=0)
    weighted = weight * shading
    after = jnp.sum(weighted, axis=1, keepdims=True) - jnp.cumsum(weighted, axis=1)
    grad_depth = shading * leaving - after - (grad_trans * leaving[:, -1])[:, None]
    grad_density = grad_depth * step_len[:, None]
    grad_sample = weight[None] * grad_colour[:, :, None]
    return (grad_density, grad_sample)


def ray_level(seg_colour, seg_trans, target):
    seg_total = seg_trans.shape[1]
    through = jnp.cumprod(seg_trans, axis=1)
    prefix = jnp.concatenate([jnp.ones_like(seg_trans[:, :1]), through[:, :-1]], axis=1)
    rendered = jnp.sum(prefix[None] * seg_colour, axis=2)
    residual = rendered - target
    grad_colour = prefix[None] * residual[:, :, None]
    behind_list = [jnp.zeros_like(rendered)]
    for offset in range(seg_total - 1, 0, -1):
        behind_list.append(seg_colour[:, :, offset] + seg_trans[:, offset][None] * behind_list[-1])
    behind = jnp.stack(behind_list[::-1], axis=2)
    grad_trans = prefix * jnp.sum(behind * residual[:, :, None], axis=0)
    return (rendered, grad_colour, grad_trans)


def output_grad(output, grad_density, grad_sample):
    colour = jax.nn.sigmoid(output[1:])
    first_row = grad_density * jax.nn.sigmoid(output[0])
    others = grad_sample * colour * (1.0 - colour)
    return jnp.concatenate([first_row[None], others], axis=0).astype(jnp.bfloat16)


def network_grad(head_local, encoded, before, hidden, upstream):
    grad_head = lax.dot_general(
        upstream, hidden, (((1,), (1,)), ((), ())), preferred_element_type=jnp.float32
    )
    grad_hidden = lax.dot_general(
        head_local, upstream, (((0,), (0,)), ((), ())), preferred_element_type=jnp.float32
    )
    logistic = jax.nn.sigmoid(before)
    grad_before = (grad_hidden * logistic * (1.0 + before * (1.0 - logistic))).astype(jnp.bfloat16)
    grad_first = lax.dot_general(
        grad_before, encoded, (((1,), (1,)), ((), ())), preferred_element_type=jnp.float32
    )
    return (grad_first, grad_head)


def by_exchange(positions, spacing, crossings, target, first_weight, head_weight):
    across = lax.axis_size(("gx", "gy"))
    along_count = lax.axis_size("gz")
    devices = across * along_count
    ray_rows = crossings.shape[0]
    entries = ray_rows * SEGS
    capacity = 2 * entries // devices
    total_slots = devices * capacity
    sample_total = total_slots * SAMPLES
    block_size = math.gcd(sample_total, BLOCK_LIMIT)
    block_count = sample_total // block_size
    block_segs = block_size // SAMPLES
    first_local = first_weight[0]
    head_local = head_weight[0]
    brick_ids = crossings.reshape(entries)
    order_rank = jnp.arange(entries, dtype=jnp.int32)
    earlier = (brick_ids[:, None] == brick_ids[None, :]) & (
        order_rank[None, :] < order_rank[:, None]
    )
    column = brick_ids * capacity + jnp.sum(earlier.astype(jnp.int32), axis=1)
    own_points = positions.reshape(3, entries, SAMPLES)
    own_steps = spacing.reshape(entries)
    send_points = jnp.zeros((3, total_slots, SAMPLES), jnp.float32).at[:, column, :].set(own_points)
    send_steps = jnp.zeros((1, total_slots), jnp.float32).at[0, column].set(own_steps)
    got_points, got_steps = (
        lax.all_to_all(
            lax.all_to_all(
                send_points.reshape(3, across, along_count, capacity * SAMPLES),
                ("gx", "gy"),
                split_axis=1,
                concat_axis=1,
                tiled=True,
            ),
            "gz",
            split_axis=2,
            concat_axis=2,
            tiled=True,
        ),
        lax.all_to_all(
            lax.all_to_all(
                send_steps.reshape(1, across, along_count, capacity),
                ("gx", "gy"),
                split_axis=1,
                concat_axis=1,
                tiled=True,
            ),
            "gz",
            split_axis=2,
            concat_axis=2,
            tiled=True,
        ),
    )
    point_blocks = got_points.reshape(3, block_count, block_size).transpose(1, 0, 2)
    step_blocks = got_steps.reshape(block_count, block_segs)

    def forward_turn(unused, inputs):
        block_points, block_steps = inputs
        encoded, before, hidden, output = network(first_local, head_local, block_points)
        density, colour = activate(output)
        result = jnp.concatenate([density[None], colour], axis=0)
        return (unused, result)

    unused, results = lax.scan(
        forward_turn, jnp.zeros((), jnp.float32), (point_blocks, step_blocks)
    )
    values = results.transpose(1, 0, 2).reshape(4, across, along_count, capacity * SAMPLES)
    returned = lax.all_to_all(
        lax.all_to_all(values, ("gx", "gy"), split_axis=1, concat_axis=1, tiled=True),
        "gz",
        split_axis=2,
        concat_axis=2,
        tiled=True,
    )
    owned = returned.reshape(4, total_slots, SAMPLES)[:, column, :]
    seg_colour, seg_trans, weight, leaving = segment_forward(owned[0], owned[1:], own_steps)
    rendered, grad_colour, grad_trans = ray_level(
        seg_colour.reshape(3, ray_rows, SEGS), seg_trans.reshape(ray_rows, SEGS), target
    )
    grad_density, grad_sample = segment_backward(
        owned[1:],
        weight,
        leaving,
        own_steps,
        grad_colour.reshape(3, entries),
        grad_trans.reshape(entries),
    )
    stacked = jnp.concatenate([grad_density[None], grad_sample], axis=0)
    send_grads = jnp.zeros((4, total_slots, SAMPLES), jnp.float32).at[:, column, :].set(stacked)
    got_grads = lax.all_to_all(
        lax.all_to_all(
            send_grads.reshape(4, across, along_count, capacity * SAMPLES),
            ("gx", "gy"),
            split_axis=1,
            concat_axis=1,
            tiled=True,
        ),
        "gz",
        split_axis=2,
        concat_axis=2,
        tiled=True,
    )
    grad_blocks = got_grads.reshape(4, block_count, block_size).transpose(1, 0, 2)

    def backward_turn(totals, inputs):
        block_points, block_steps, block_upstream = inputs
        encoded, before, hidden, output = network(first_local, head_local, block_points)
        grad_density = block_upstream[0]
        grad_sample = block_upstream[1:]
        upstream = output_grad(output, grad_density, grad_sample)
        grad_first, grad_head = network_grad(head_local, encoded, before, hidden, upstream)
        return ((totals[0] + grad_first, totals[1] + grad_head), None)

    start_totals = (
        jnp.zeros(first_local.shape, jnp.float32),
        jnp.zeros(head_local.shape, jnp.float32),
    )
    totals, unused_out = lax.scan(
        backward_turn, start_totals, (point_blocks, step_blocks, grad_blocks)
    )
    grad_first, grad_head = totals
    square_sum = jnp.sum(grad_first * grad_first) + jnp.sum(grad_head * grad_head)
    overall = lax.psum(square_sum, ("gx", "gy", "gz"))
    count_all = devices * (grad_first.size + grad_head.size)
    scale = lax.rsqrt(overall / count_all + NORM_EPS)
    return (rendered, (grad_first * scale)[None], (grad_head * scale)[None])


def solution(mesh):
    in_specs = (
        P(None, ("gx", "gy", "gz"), None),
        P(("gx", "gy", "gz"), None),
        P(("gx", "gy", "gz"), None),
        P(None, ("gx", "gy", "gz")),
        P(("gx", "gy", "gz"), None, None),
        P(("gx", "gy", "gz"), None, None),
    )
    out_specs = (
        P(None, ("gx", "gy", "gz")),
        P(("gx", "gy", "gz"), None, None),
        P(("gx", "gy", "gz"), None, None),
    )
    body = by_gather if mesh.size <= GATHER_LIMIT else by_exchange
    return jax.shard_map(
        body, mesh=mesh, in_specs=in_specs, out_specs=out_specs, check_vma=False
    )
```
